128 devices in a mesh: seq: 32 (over x, y, z_hi), dp: 4 (over z_lo, core).
Axes of the slice: x: 4, y: 4, z: 4 (z_hi: 2, z_lo: 2; z = z_hi * 2 + z_lo), core: 2. Of those that a mesh axis runs over, the one named last changes fastest.
Arguments:
- hidden: bfloat16 [4, 4096, 4096], P('dp', 'seq'), may hold values from -6 to 6
- queries: bfloat16 [4, 4096, 4096], P('dp', 'seq'), may hold values from -122 to 122
- keyvals: bfloat16 [4, 4096, 512], P('dp', 'seq'), may hold values from -5 to 5
- out_grad: bfloat16 [4, 4096, 4096], P('dp', 'seq'), may hold values from -6 to 6
- segment: int32 [4, 4096], P('dp', 'seq'), may hold values from 0 to 2, never falling along the last dimension, each value on 1 to 3072 neighbouring positions
Outputs:
- query_grad: bfloat16 [4, 4096, 4096], P('dp', 'seq')
- keyval_grad: bfloat16 [4, 4096, 512], P('dp', 'seq')
- weight_grad: float32 [4096, 512], P(('seq', 'dp'))
The draws below stay inside these ranges and needn't reach their ends.
All inputs are finite; a program needn't handle non-finite values.
Results may differ from the reference program's by a relative error of at most 0.02.
Values may be sent and summed in bfloat16 or wider, within the bound.
No kernel may reach another device: no remote copies, remote signals or barrier semaphores. Data moves between devices by JAX's collectives and lax.ppermute only.
A program may use at most 128 MiB of HBM per device.

```python
import math
import jax
import jax.numpy as jnp
import numpy as np
from jax import lax

D = 4096
HQ = 32
HK = 2
DH = 128
S = 4096
ROWS = 4


def base_keys(key):
    return jnp.clip(jax.random.normal(key, (ROWS, S, HK * DH), jnp.float32), -4.5, 4.5)


def draw_keyvals(key, part):
    keys = base_keys(key)
    key = jax.random.fold_in(key, 11)
    values = jnp.clip(jax.random.normal(key, (ROWS, S, HK * DH), jnp.float32), -4.5, 4.5)
    return jnp.concatenate([keys, values], axis=-1).astype(jnp.bfloat16)


def draw_queries(key, part):
    key = jax.random.fold_in(key, 7)
    first = jax.random.fold_in(key, 0)
    result = jnp.clip(jax.random.normal(first, (ROWS, S, HQ, DH), jnp.float32), -4.5, 4.5)
    return result.reshape(ROWS, S, HQ * DH).astype(jnp.bfloat16)


def with_spikes(array, stream_key, source, target, shards_of, factor):
    def block_of(position):
        return (jnp.arange(array.shape[position]) // (array.shape[position] // shards_of)).reshape((-1,) + (1,) * (array.ndim - 1 - position))

    one_side = jax.random.permutation(stream_key, shards_of)[block_of(target)]
    second = (block_of(target) + shards_of // 2) % shards_of
    return jnp.where((block_of(source) == one_side) | (block_of(source) == second), factor * array, array)


def block_levels(stream_key, extent, shards, smallest, top_value):
    factor_of, own = 1.0, jax.random.fold_in(stream_key, 6)
    for axis_at, shards_of in shards:
        heights = jnp.exp(jax.random.uniform(jax.random.fold_in(own, axis_at), (shards_of,), jnp.float32, smallest / len(shards), top_value / len(shards)))
        factor_of = factor_of * jnp.repeat(heights, extent[axis_at] // shards_of).reshape([-1 if axis == axis_at else 1 for axis in range(len(extent))])
    return factor_of


def profile(amount, total, limit, skew):
    portions = [(1 << 20) // math.isqrt(standing ** skew) + 1 for standing in range(2, amount + 1)]
    spare, counts = total - limit - (amount - 1), [1] * (amount - 1)
    while spare > 0:
        candidates = [i for i in range(amount - 1) if counts[i] < limit]
        whole, budget = sum([portions[i] for i in candidates]), spare
        for i in candidates:
            addition = min(limit - counts[i], max(1, budget * portions[i] // whole), spare)
            counts[i] = counts[i] + addition
            spare = spare - addition
    return np.array([limit] + counts)


def uneven_parts(rng, amount, total, reach, slope):
    if amount == 2:
        one = jax.random.randint(rng, (), max(1, total - reach), min(reach, total - 1) + 1)
        return jnp.stack([one, total - one])
    tallies = jnp.asarray(profile(amount, total, reach, slope), jnp.int32)
    couples = (amount - 1) // 2
    donor, sink = tallies[1:1 + 2 * couples:2], tallies[2:2 + 2 * couples:2]
    room = jnp.minimum(donor - 1, reach - sink)
    shifted = jax.random.randint(jax.random.fold_in(rng, 1), (couples,), 0, 1 << 20) % (room + 1)
    tallies = tallies.at[1:1 + 2 * couples:2].set(donor - shifted).at[2:2 + 2 * couples:2].set(sink + shifted)
    return tallies[jax.random.permutation(jax.random.fold_in(rng, 2), amount)]


def centred(key, shape, deviation, limit, shards=(), held_as=jnp.bfloat16):
    array = deviation * jax.random.normal(key, shape, jnp.float32)
    if shards:
        array = array * block_levels(key, shape, shards, -0.22, 0.18)
    return jnp.clip(array, -limit, limit).astype(held_as)


def bell_draw_with(key, shape, scale, bound, shards, heavy, kind=jnp.bfloat16):
    array = scale * jax.random.normal(key, shape, jnp.float32)
    if shards:
        array = array * block_levels(key, shape, shards, -0.22, 0.18)
    return jnp.clip(with_spikes(array, jax.random.fold_in(key, 3), *heavy), -bound, bound).astype(kind)


def setup_inputs(seed: int = 0) -> dict:
    key_of = jax.random.split(jax.random.key(seed), 6)
    return {
        "hidden": bell_draw_with(key_of[0], (ROWS, S, D), 1.0, 6.0, ((0, 4), (1, 32)), (1, 2, 32, 2.75)),
        "queries": draw_queries(jax.random.fold_in(key_of[5], 71), 0),
        "keyvals": draw_keyvals(jax.random.fold_in(key_of[5], 71), 0),
        "out_grad": centred(key_of[3], (ROWS, S, HQ * DH), 1.0, 6.0, ((0, 4), (1, 32))),
        "segment": jax.vmap(lambda own: jnp.searchsorted(jnp.cumsum(uneven_parts(own, 3, S, 3 * S // 4, 0)), jnp.arange(S), side="right"))(jax.random.split(key_of[4], ROWS)).reshape((ROWS, S)).astype(jnp.int32),
    }


MASKED = -1e30


def row_grads(query_row, keyval_row, grad_row, segment_row):
    groups = HQ // HK
    scale = DH ** -0.5
    keys = keyval_row[:, :HK * DH].reshape(S, HK, DH).astype(jnp.float32)
    values = keyval_row[:, HK * DH:].reshape(S, HK, DH).astype(jnp.float32)
    places = jnp.arange(S, dtype=jnp.int32)
    block = min(S, 512)
    count = S // block

    def step(carry, index):
        key_acc, value_acc = carry
        first = (index * block).astype(jnp.int32)
        query = lax.dynamic_slice_in_dim(query_row, first, block, 0).reshape(block, HK, groups, DH).astype(jnp.float32)
        cotan = lax.dynamic_slice_in_dim(grad_row, first, block, 0).reshape(block, HK, groups, DH).astype(jnp.float32)
        qseg = lax.dynamic_slice_in_dim(segment_row, first, block, 0)
        qpos = first + jnp.arange(block, dtype=jnp.int32)
        allowed = (qseg[:, None] == segment_row[None, :]) & (places[None, :] <= qpos[:, None])
        scores = jnp.einsum('qhgd,khd->hgqk', query, keys) * scale
        top = jnp.max(jnp.where(allowed, scores, MASKED), axis=-1)
        weights = jnp.where(allowed, jnp.exp(scores - top[..., None]), 0.0)
        total = jnp.sum(weights, axis=-1)
        rounded = lax.optimization_barrier(weights.astype(jnp.bfloat16)).astype(jnp.float32)
        attended = jnp.einsum('hgqk,khd->qhgd', rounded, values) / jnp.transpose(total, (2, 0, 1))[..., None]
        log_total = top + jnp.log(total)
        delta = jnp.transpose(jnp.sum(cotan * attended, axis=-1), (1, 2, 0))
        again = jnp.where(allowed, jnp.exp(scores - log_total[..., None]), 0.0)
        again16 = lax.optimization_barrier(again.astype(jnp.bfloat16)).astype(jnp.float32)
        value_acc = value_acc + jnp.einsum('hgqk,qhgd->khd', again16, cotan)
        dprob = jnp.einsum('qhgd,khd->hgqk', cotan, values)
        dscore = again * (dprob - delta[..., None])
        dscore16 = lax.optimization_barrier(dscore.astype(jnp.bfloat16)).astype(jnp.float32)
        query_part = jnp.einsum('hgqk,khd->qhgd', dscore16, keys) * scale
        key_acc = key_acc + jnp.einsum('hgqk,qhgd->khd', dscore16, query) * scale
        return (key_acc, value_acc), query_part.reshape(block, HQ * DH)

    start_acc = jnp.zeros((S, HK, DH), jnp.float32)
    (key_acc, value_acc), parts = lax.scan(step, (start_acc, start_acc), jnp.arange(count, dtype=jnp.int32))
    query_grad = parts.reshape(S, HQ * DH).astype(jnp.bfloat16)
    keyval_grad = jnp.concatenate([key_acc.reshape(S, HK * DH), value_acc.reshape(S, HK * DH)], axis=-1).astype(jnp.bfloat16)
    return query_grad, keyval_grad


def reference(hidden, queries, keyvals, out_grad, segment):
    query_list = []
    keyval_list = []
    weight_grad = jnp.zeros((D, 2 * HK * DH), jnp.float32)
    for row in range(ROWS):
        query_grad, keyval_grad = row_grads(queries[row], keyvals[row], out_grad[row], segment[row])
        query_list.append(query_grad)
        keyval_list.append(keyval_grad)
        weight_grad = weight_grad + jnp.dot(hidden[row].T, keyval_grad, preferred_element_type=jnp.float32)
    return jnp.stack(query_list), jnp.stack(keyval_list), weight_grad
```

```python
import jax
import jax.numpy as jnp
from jax import lax
from jax.experimental import pallas as pl
from jax.experimental.pallas import tpu as pltpu
from jax.sharding import PartitionSpec as P

HQ = 32
HK = 2
DH = 128
SCALE = DH ** -0.5
EXP2_SCALE = SCALE * 1.4426950408889634
MASKED = -1e30
LOWEST = -1e29
SEGMENT_ROWS = 16
BQ = 512
BK = 512
NT = (((1,), (1,)), ((), ()))
NN = (((1,), (0,)), ((), ()))
TN = (((0,), (0,)), ((), ()))

def dot(a, b, dims):
    return lax.dot_general(a, b, dims, preferred_element_type=jnp.float32)

def attention_kernel(x_ref, dq_ref, dkv_ref, p_ref, dp_ref, m_ref, dk_ref, dv_ref):
    blocks = x_ref.shape[0]
    seq = blocks * 128
    qn, kn = BQ // 128, BK // 128

    def rows(first, count, slot):
        return x_ref[pl.ds(first, count), slot * 128 : (slot + 1) * 128, :].reshape(count * 128, DH)

    segments = x_ref[:, 512:513, :].astype(jnp.float32)
    count0 = jnp.sum(jnp.where(segments < 0.5, 1.0, 0.0)).astype(jnp.int32)
    count1 = jnp.sum(jnp.where(segments < 1.5, 1.0, 0.0)).astype(jnp.int32)

    def start_of(pos):
        return jnp.where(pos >= count1, count1, jnp.where(pos >= count0, count0, 0))

    dk_ref[...] = jnp.zeros_like(dk_ref)
    dv_ref[...] = jnp.zeros_like(dv_ref)

    def query_block(i, _):
        first = i * BQ
        q = rows(i * qn, qn, 0)
        cotan = rows(i * qn, qn, 1)
        qpos = first + lax.broadcasted_iota(jnp.int32, (1, BQ), 1)
        qstart = start_of(qpos)
        low = start_of(first) // BK
        high = (first + BQ - 1) // BK + 1
        last_start = start_of(first + BQ - 1)

        def scores(kb, carry, masked):
            top, total, delta = carry
            k = rows(kb * kn, kn, 2)
            v = rows(kb * kn, kn, 3)
            st = dot(k, q, NT)
            dpt = dot(v, cotan, NT)
            if masked:
                kpos = kb * BK + lax.broadcasted_iota(jnp.int32, (BK, BQ), 0)
                st = jnp.where((kpos >= qstart) & (kpos <= qpos), st, MASKED)
            newtop = jnp.maximum(top, jnp.max(st, axis=0, keepdims=True))
            p = jnp.exp2((st - newtop) * EXP2_SCALE)
            fade = jnp.exp2((top - newtop) * EXP2_SCALE)
            total = total * fade + jnp.sum(p, axis=0, keepdims=True)
            delta = delta * fade + jnp.sum(p * dpt, axis=0, keepdims=True)
            at = pl.ds(pl.multiple_of(kb * BK, BK), BK)
            p_ref[at, :] = p
            dp_ref[at, :] = dpt
            m_ref[pl.ds(kb, 1), :] = newtop
            return newtop, total, delta

        def step(kb, carry):
            plain = ((kb + 1) * BK - 1 <= first) & (kb * BK >= last_start)
            return lax.cond(plain, lambda c: scores(kb, c, False), lambda c: scores(kb, c, True), carry)

        zero = jnp.zeros((1, BQ), jnp.float32)
        top, total, delta = lax.fori_loop(low, high, step, (zero + LOWEST, zero, zero))
        inverse = 1.0 / total
        delta = delta * inverse

        def grads(kb, dq):
            k = rows(kb * kn, kn, 2)
            at = pl.ds(pl.multiple_of(kb * BK, BK), BK)
            factor = jnp.exp2((m_ref[pl.ds(kb, 1), :] - top) * EXP2_SCALE) * inverse
            w = p_ref[at, :] * factor
            ds = (w * (dp_ref[at, :] - delta)).astype(jnp.bfloat16)
            dv_ref[at, :] += dot(w.astype(jnp.bfloat16), cotan, NN)
            dk_ref[at, :] += dot(ds, q, NN)
            return dq + dot(ds, k, TN)

        dq = lax.fori_loop(low, high, grads, jnp.zeros((BQ, DH), jnp.float32))
        dq_ref[pl.ds(i * qn, qn)] = (dq * SCALE).astype(jnp.bfloat16).reshape(qn, 128, DH)
        return 0

    lax.fori_loop(0, seq // BQ, query_block, 0)

    def finish(b, _):
        at = pl.ds(pl.multiple_of(b * 128, 128), 128)
        dkv_ref[b, :128, :] = (dk_ref[at, :] * SCALE).astype(jnp.bfloat16)
        dkv_ref[b, 128:, :] = dv_ref[at, :].astype(jnp.bfloat16)
        return 0

    lax.fori_loop(0, blocks, finish, 0)

def attention(x):
    blocks = x.shape[0]
    seq = blocks * 128
    spec = pl.BlockSpec(memory_space=pltpu.VMEM)
    return pl.pallas_call(
        attention_kernel,
        out_shape=(
            jax.ShapeDtypeStruct((blocks, 128, DH), jnp.bfloat16),
            jax.ShapeDtypeStruct((blocks, 256, DH), jnp.bfloat16),
        ),
        in_specs=[spec],
        out_specs=(spec, spec),
        scratch_shapes=[
            pltpu.VMEM((seq, BQ), jnp.float32),
            pltpu.VMEM((seq, BQ), jnp.float32),
            pltpu.VMEM((max(8,seq // BK), BQ), jnp.float32),
            pltpu.VMEM((seq, DH), jnp.float32),
            pltpu.VMEM((seq, DH), jnp.float32),
        ],
        compiler_params=pltpu.CompilerParams(vmem_limit_bytes=40 * 1024 * 1024),
        name="attention",
    )(x)


def shards(hidden, queries, keyvals, out_grad, segment):
    seq, dp = lax.axis_size("seq"), lax.axis_size("dp")
    tokens, width = hidden.shape[1], hidden.shape[2]
    groups = HQ // HK

    def by_head(array):
        return jnp.transpose(array.reshape(tokens, HQ, DH), (1, 0, 2))

    kv = jnp.transpose(keyvals[0].reshape(tokens, 2 * HK, DH), (1, 0, 2))
    numbers = segment[0].astype(jnp.bfloat16)
    send = jnp.concatenate(
        [
            by_head(queries[0]),
            by_head(out_grad[0]),
            jnp.repeat(kv[:HK], groups, axis=0),
            jnp.repeat(kv[HK:], groups, axis=0),
            jnp.broadcast_to(numbers, (HQ, SEGMENT_ROWS, tokens)),
        ],
        axis=1,
    )
    mine = lax.all_to_all(send, "seq", split_axis=0, concat_axis=0, tiled=True)

    share = width // (seq * dp)
    columns = jnp.transpose(hidden[0].T.reshape(seq, dp, share, tokens), (1, 0, 2, 3))
    columns = columns.reshape(dp, seq * share, tokens)
    columns = lax.all_to_all(columns, "dp", split_axis=0, concat_axis=0, tiled=True)

    dq, dkv = attention(mine)
    dkv = lax.all_to_all(dkv, "seq", split_axis=0, concat_axis=0, tiled=True)
    dq = lax.all_to_all(dq, "seq", split_axis=0, concat_axis=0, tiled=True)
    query_grad = jnp.transpose(dq, (1, 0, 2)).reshape(tokens, HQ * DH)

    total = jnp.sum(dkv.reshape(HK, groups, 2, tokens, DH).astype(jnp.float32), axis=1)
    keyval_grad = jnp.transpose(total, (2, 1, 0, 3)).reshape(tokens, 2 * HK * DH)
    keyval_grad = keyval_grad.astype(jnp.bfloat16)

    every = lax.all_gather(keyval_grad, "dp", axis=0)
    partial = jnp.einsum("sdt,stc->dc", columns, every, preferred_element_type=jnp.float32)
    partial = partial.astype(jnp.bfloat16).reshape(seq, share, 2 * HK * DH)
    partial = lax.all_to_all(partial, "seq", split_axis=0, concat_axis=0, tiled=True)
    weight_grad = jnp.sum(partial.astype(jnp.float32), axis=0)
    return (query_grad[None], keyval_grad[None], weight_grad)


def solution(mesh):
    in_specs = (
        P("dp", "seq", None),
        P("dp", "seq", None),
        P("dp", "seq", None),
        P("dp", "seq", None),
        P("dp", "seq"),
    )
    out_specs = (P("dp", "seq", None), P("dp", "seq", None), P(("seq", "dp"), None))
    return jax.shard_map(shards, mesh=mesh, in_specs=in_specs, out_specs=out_specs, check_vma=False)
```

```python
import jax
import jax.numpy as jnp
from jax import lax
from jax.experimental import pallas as pl
from jax.experimental.pallas import tpu as pltpu
from jax.sharding import PartitionSpec as P

HQ = 32
HK = 2
DH = 128
SCALE = DH ** -0.5
EXP2_SCALE = SCALE * 1.4426950408889634
MASKED = -1e30
LOWEST = -1e29
SEGMENT_ROWS = 16
BQ = 512
UNIT = 512
CHUNKS = (4, 2, 1)
VMEM_LIMIT = 48 * 1024 * 1024
NT = (((1,), (1,)), ((), ()))
NN = (((1,), (0,)), ((), ()))
TN = (((0,), (0,)), ((), ()))


def dot(a, b, dims):
    return lax.dot_general(a, b, dims, preferred_element_type=jnp.float32)


def attention_kernel(x_ref, out_ref, p_ref, dp_ref, m_ref, dk_ref, dv_ref):
    blocks = x_ref.shape[0]
    seq = blocks * 128
    qn, un = BQ // 128, UNIT // 128

    def rows(first, count, slot):
        part = x_ref[pl.ds(first, count), slot * 128 : (slot + 1) * 128, :]
        return part.reshape(count * 128, DH)

    segments = x_ref[:, 512:513, :].astype(jnp.float32)
    count0 = jnp.sum(jnp.where(segments < 0.5, 1.0, 0.0)).astype(jnp.int32)
    count1 = jnp.sum(jnp.where(segments < 1.5, 1.0, 0.0)).astype(jnp.int32)

    def start_of(pos):
        return jnp.where(pos >= count1, count1, jnp.where(pos >= count0, count0, 0))

    dk_ref[...] = jnp.zeros_like(dk_ref)
    dv_ref[...] = jnp.zeros_like(dv_ref)

    def query_block(i, _):
        first = i * BQ
        q = rows(i * qn, qn, 0)
        cotan = rows(i * qn, qn, 1)
        qpos = first + lax.broadcasted_iota(jnp.int32, (1, BQ), 1)
        qstart = start_of(qpos)
        low = start_of(first) // UNIT
        high = (first + BQ - 1) // UNIT + 1

        def walk(body, state):
            at = low
            for size in CHUNKS:
                count = (high - at) // size

                def step(t, carry, size=size, at=at):
                    return body(at + t * size, size, carry)

                state = lax.fori_loop(0, count, step, state)
                at = at + count * size
            return state

        def scores(kb, size, carry):
            top, total, delta = carry
            k = rows(kb * un, size * un, 2)
            v = rows(kb * un, size * un, 3)
            st = dot(k, q, NT)
            dpt = dot(v, cotan, NT)
            at = pl.ds(pl.multiple_of(kb * UNIT, UNIT), size * UNIT)
            kpos = kb * UNIT + lax.broadcasted_iota(jnp.int32, (size * UNIT, BQ), 0)
            st = jnp.where((kpos >= qstart) & (kpos <= qpos), st, MASKED)
            newtop = jnp.maximum(top, jnp.max(st, axis=0, keepdims=True))
            p = jnp.exp2((st - newtop) * EXP2_SCALE)
            fade = jnp.exp2((top - newtop) * EXP2_SCALE)
            total = total * fade + jnp.sum(p, axis=0, keepdims=True)
            delta = delta * fade + jnp.sum(p * dpt, axis=0, keepdims=True)
            p_ref[at, :] = p
            dp_ref[at, :] = dpt
            m_ref[pl.ds(kb, 1), :] = newtop
            return newtop, total, delta

        zero = jnp.zeros((1, BQ), jnp.float32)
        top, total, delta = walk(scores, (zero + LOWEST, zero, zero))
        inverse = 1.0 / total
        delta = delta * inverse

        def grads(kb, size, dq):
            k = rows(kb * un, size * un, 2)
            at = pl.ds(pl.multiple_of(kb * UNIT, UNIT), size * UNIT)
            factor = jnp.exp2((m_ref[pl.ds(kb, 1), :] - top) * EXP2_SCALE) * inverse
            w = p_ref[at, :] * factor
            ds = (w * (dp_ref[at, :] - delta)).astype(jnp.bfloat16)
            dv_ref[at, :] += dot(w.astype(jnp.bfloat16), cotan, NN)
            dk_ref[at, :] += dot(ds, q, NN)
            return dq + dot(ds, k, TN)

        dq = walk(grads, jnp.zeros((BQ, DH), jnp.float32))
        out_ref[pl.ds(i * qn, qn), :128, :] = (
            (dq * SCALE).astype(jnp.bfloat16).reshape(qn, 128, DH)
        )
        return 0

    lax.fori_loop(0, seq // BQ, query_block, 0)

    def finish(b, _):
        at = pl.ds(pl.multiple_of(b * 128, 128), 128)
        out_ref[b, 128:256, :] = (dk_ref[at, :] * SCALE).astype(jnp.bfloat16)
        out_ref[b, 256:384, :] = dv_ref[at, :].astype(jnp.bfloat16)
        return 0

    lax.fori_loop(0, blocks, finish, 0)


def in_vmem(body, out_shape, inputs, scratch=(), name=None):
    spec = pl.BlockSpec(memory_space=pltpu.VMEM)
    many = isinstance(out_shape, tuple)
    return pl.pallas_call(
        body,
        out_shape=out_shape,
        in_specs=[spec] * len(inputs),
        out_specs=(spec,) * len(out_shape) if many else spec,
        scratch_shapes=list(scratch),
        compiler_params=pltpu.CompilerParams(vmem_limit_bytes=VMEM_LIMIT),
        name=name,
    )(*inputs)


def attention(x):
    blocks = x.shape[0]
    seq = blocks * 128
    scratch = [
        pltpu.VMEM((seq, BQ), jnp.float32),
        pltpu.VMEM((seq, BQ), jnp.float32),
        pltpu.VMEM((seq // UNIT, BQ), jnp.float32),
        pltpu.VMEM((seq, DH), jnp.float32),
        pltpu.VMEM((seq, DH), jnp.float32),
    ]
    out = jax.ShapeDtypeStruct((blocks, 384, DH), jnp.bfloat16)
    return in_vmem(attention_kernel, out, [x], scratch, "attention")


def pack_kernel(q_ref, g_ref, kv_ref, seg_ref, h_ref, send_ref, cols_ref):
    tokens = q_ref.shape[0]
    groups = HQ // HK
    dp, width = cols_ref.shape[0], cols_ref.shape[1]
    share = h_ref.shape[1] // (HQ * dp)
    numbers = jnp.broadcast_to(seg_ref[...].astype(jnp.bfloat16), (SEGMENT_ROWS, tokens))
    for h in range(HQ):
        at = slice(h * DH, (h + 1) * DH)
        k = (h // groups) * DH
        v = HK * DH + k
        send_ref[h, 0:128, :] = q_ref[:, at]
        send_ref[h, 128:256, :] = g_ref[:, at]
        send_ref[h, 256:384, :] = kv_ref[:, k : k + DH]
        send_ref[h, 384:512, :] = kv_ref[:, v : v + DH]
        send_ref[h, 512:528, :] = numbers
    span = share * dp
    for s in range(width // share):
        turned = h_ref[:, s * span : (s + 1) * span].T
        for r in range(dp):
            cols_ref[r, s * share : (s + 1) * share, :] = turned[r * share : (r + 1) * share]


def combine_kernel(part_ref, out_ref):
    groups = HQ // HK
    for g in range(HK):
        for kind in range(2):
            total = jnp.zeros((128, DH), jnp.float32)
            for h in range(g * groups, (g + 1) * groups):
                total += part_ref[h, (kind + 1) * 128 : (kind + 2) * 128, :].astype(jnp.float32)
            at = (kind * HK + g) * DH
            out_ref[:, at : at + DH] = total.astype(jnp.bfloat16)


def weight_kernel(cols_ref, kv_ref, out_ref):
    seq, share = out_ref.shape[0], out_ref.shape[1]
    total = dot(cols_ref[0], kv_ref[0], NN)
    for r in range(1, cols_ref.shape[0]):
        total += dot(cols_ref[r], kv_ref[r], NN)
    out_ref[...] = total.astype(jnp.bfloat16).reshape(seq, share, total.shape[1])


def unpack_kernel(part_ref, out_ref):
    for h in range(HQ):
        out_ref[:, h * DH : (h + 1) * DH] = part_ref[h, :128, :]


def total_kernel(part_ref, out_ref):
    total = part_ref[0].astype(jnp.float32)
    for s in range(1, part_ref.shape[0]):
        total += part_ref[s].astype(jnp.float32)
    out_ref[...] = total


def exchange(array, axis):
    return lax.all_to_all(array, axis, split_axis=0, concat_axis=0, tiled=True)


def shards(hidden, queries, keyvals, out_grad, segment):
    seq, dp = lax.axis_size("seq"), lax.axis_size("dp")
    tokens, width = hidden.shape[1], hidden.shape[2]
    share = width // (seq * dp)
    half = jnp.bfloat16
    shape = jax.ShapeDtypeStruct

    send, columns = in_vmem(
        pack_kernel,
        (shape((HQ, 4 * tokens + SEGMENT_ROWS, DH), half), shape((dp, seq * share, tokens), half)),
        [queries[0], out_grad[0], keyvals[0], segment, hidden[0]],
        name="pack",
    )
    mine = exchange(send, "seq")
    columns = exchange(columns, "dp")
    back = exchange(attention(mine), "seq")
    keyval_grad = in_vmem(
        combine_kernel, shape((tokens, 2 * HK * DH), half), [back], name="combine"
    )
    every = lax.all_gather(keyval_grad, "dp", axis=0)
    partial = in_vmem(
        weight_kernel, shape((seq, share, 2 * HK * DH), half), [columns, every], name="weight"
    )
    partial = exchange(partial, "seq")
    query_grad = in_vmem(unpack_kernel, shape((tokens, HQ * DH), half), [back], name="unpack")
    weight_grad = in_vmem(
        total_kernel, shape((share, 2 * HK * DH), jnp.float32), [partial], name="total"
    )
    return (query_grad[None], keyval_grad[None], weight_grad)


def solution(mesh):
    in_specs = (
        P("dp", "seq", None),
        P("dp", "seq", None),
        P("dp", "seq", None),
        P("dp", "seq", None),
        P("dp", "seq"),
    )
    out_specs = (P("dp", "seq", None), P("dp", "seq", None), P(("seq", "dp"), None))
    return jax.shard_map(shards, mesh=mesh, in_specs=in_specs, out_specs=out_specs, check_vma=False)
```

```python
import jax
import jax.numpy as jnp
from jax import lax
from jax.experimental import pallas as pl
from jax.experimental.pallas import tpu as pltpu
from jax.sharding import PartitionSpec as P

HQ = 32
HK = 2
DH = 128
SCALE = DH ** -0.5
EXP2_SCALE = SCALE * 1.4426950408889634
MASKED = -1e30
LOWEST = -1e29
SEGMENT_ROWS = 16
BQ = 512
UNIT = 512
CHUNKS = (4, 2, 1)
VMEM_LIMIT = 127 * 512 * 1024
NT = (((1,), (1,)), ((), ()))
NN = (((1,), (0,)), ((), ()))
TN = (((0,), (0,)), ((), ()))


def dot(a, b, dims):
    return lax.dot_general(a, b, dims, preferred_element_type=jnp.float32)


def attention_kernel(
    x_hbm, out_hbm, x_ref, out_ref, p_ref, dp_ref, m_ref, dk_ref, dv_ref, sems, out_sems
):
    blocks = x_ref.shape[0]
    seq = blocks * 128
    qn, un = BQ // 128, UNIT // 128
    steps = seq // BQ

    def arrival(i):
        at = pl.ds(i * qn, qn)
        return pltpu.make_async_copy(x_hbm.at[at, :512], x_ref.at[at, :512], sems.at[i])

    def departure(i):
        at = pl.ds(i * qn, qn)
        return pltpu.make_async_copy(
            out_ref.at[at, :128], out_hbm.at[at, :128], out_sems.at[i]
        )

    def final(i):
        at = pl.ds(i * qn, qn)
        return pltpu.make_async_copy(
            out_ref.at[at, 128:], out_hbm.at[at, 128:], out_sems.at[steps + i]
        )

    numbers = pltpu.make_async_copy(x_hbm.at[:, 512:], x_ref.at[:, 512:], sems.at[steps])
    numbers.start()
    for i in range(steps):
        arrival(i).start()
    dk_ref[...] = jnp.zeros_like(dk_ref)
    dv_ref[...] = jnp.zeros_like(dv_ref)
    numbers.wait()

    def rows(first, count, slot):
        part = x_ref[pl.ds(first, count), slot * 128 : (slot + 1) * 128, :]
        return part.reshape(count * 128, DH)

    segments = x_ref[:, 512:513, :].astype(jnp.float32)
    count0 = jnp.sum(jnp.where(segments < 0.5, 1.0, 0.0)).astype(jnp.int32)
    count1 = jnp.sum(jnp.where(segments < 1.5, 1.0, 0.0)).astype(jnp.int32)

    def start_of(pos):
        return jnp.where(pos >= count1, count1, jnp.where(pos >= count0, count0, 0))

    def query_block(i, _):
        arrival(i).wait()
        first = i * BQ
        q = rows(i * qn, qn, 0)
        cotan = rows(i * qn, qn, 1)
        qpos = first + lax.broadcasted_iota(jnp.int32, (1, BQ), 1)
        qstart = start_of(qpos)
        low = start_of(first) // UNIT
        high = (first + BQ - 1) // UNIT + 1

        def walk(body, state):
            at = low
            for size in CHUNKS:
                count = (high - at) // size

                def step(t, carry, size=size, at=at):
                    return body(at + t * size, size, carry)

                state = lax.fori_loop(0, count, step, state)
                at = at + count * size
            return state

        def scores(kb, size, carry):
            top, total, delta = carry
            k = rows(kb * un, size * un, 2)
            v = rows(kb * un, size * un, 3)
            st = dot(k, q, NT)
            dpt = dot(v, cotan, NT)
            at = pl.ds(pl.multiple_of(kb * UNIT, UNIT), size * UNIT)
            kpos = kb * UNIT + lax.broadcasted_iota(jnp.int32, (size * UNIT, BQ), 0)
            st = jnp.where((kpos >= qstart) & (kpos <= qpos), st, MASKED)
            newtop = jnp.maximum(top, jnp.max(st, axis=0, keepdims=True))
            p = jnp.exp2((st - newtop) * EXP2_SCALE)
            fade = jnp.exp2((top - newtop) * EXP2_SCALE)
            total = total * fade + jnp.sum(p, axis=0, keepdims=True)
            delta = delta * fade + jnp.sum(p * dpt, axis=0, keepdims=True)
            p_ref[at, :] = p
            dp_ref[at, :] = dpt
            m_ref[pl.ds(kb, 1), :] = newtop
            return newtop, total, delta

        zero = jnp.zeros((1, BQ), jnp.float32)
        top, total, delta = walk(scores, (zero + LOWEST, zero, zero))
        inverse = 1.0 / total
        delta = delta * inverse

        def grads(kb, size, dq):
            k = rows(kb * un, size * un, 2)
            at = pl.ds(pl.multiple_of(kb * UNIT, UNIT), size * UNIT)
            factor = jnp.exp2((m_ref[pl.ds(kb, 1), :] - top) * EXP2_SCALE) * inverse
            w = p_ref[at, :] * factor
            ds = (w * (dp_ref[at, :] - delta)).astype(jnp.bfloat16)
            dv_ref[at, :] += dot(w.astype(jnp.bfloat16), cotan, NN)
            dk_ref[at, :] += dot(ds, q, NN)
            return dq + dot(ds, k, TN)

        dq = walk(grads, jnp.zeros((BQ, DH), jnp.float32))
        out_ref[pl.ds(i * qn, qn), :128, :] = (
            (dq * SCALE).astype(jnp.bfloat16).reshape(qn, 128, DH)
        )
        departure(i).start()
        return 0

    lax.fori_loop(0, steps, query_block, 0)

    def finish(i, _):
        for b in range(qn):
            at = pl.ds(pl.multiple_of((i * qn + b) * 128, 128), 128)
            out_ref[i * qn + b, 128:256, :] = (dk_ref[at, :] * SCALE).astype(jnp.bfloat16)
            out_ref[i * qn + b, 256:384, :] = dv_ref[at, :].astype(jnp.bfloat16)
        final(i).start()
        return 0

    lax.fori_loop(0, steps, finish, 0)
    for i in range(steps):
        departure(i).wait()
        final(i).wait()


def local(body, out_shape, inputs, scratch, name):
    spec = pl.BlockSpec(memory_space=pltpu.HBM)
    many = isinstance(out_shape, tuple)
    return pl.pallas_call(
        body,
        out_shape=out_shape,
        in_specs=[spec] * len(inputs),
        out_specs=(spec,) * len(out_shape) if many else spec,
        scratch_shapes=scratch,
        compiler_params=pltpu.CompilerParams(vmem_limit_bytes=VMEM_LIMIT),
        name=name,
    )(*inputs)


def attention(x):
    blocks = x.shape[0]
    seq = blocks * 128
    return pl.pallas_call(
        attention_kernel,
        out_shape=jax.ShapeDtypeStruct((blocks, 384, DH), jnp.bfloat16),
        in_specs=[pl.BlockSpec(memory_space=pltpu.HBM)],
        out_specs=pl.BlockSpec(memory_space=pltpu.HBM),
        scratch_shapes=[
            pltpu.VMEM(x.shape, jnp.bfloat16),
            pltpu.VMEM((blocks, 384, DH), jnp.bfloat16),
            pltpu.VMEM((seq, BQ), jnp.float32),
            pltpu.VMEM((seq, BQ), jnp.float32),
            pltpu.VMEM((seq // UNIT, BQ), jnp.float32),
            pltpu.VMEM((seq, DH), jnp.float32),
            pltpu.VMEM((seq, DH), jnp.float32),
            pltpu.SemaphoreType.DMA((seq // BQ + 1,)),
            pltpu.SemaphoreType.DMA((2 * seq // BQ,)),
        ],
        compiler_params=pltpu.CompilerParams(vmem_limit_bytes=VMEM_LIMIT),
        cost_estimate=pl.CostEstimate(
            flops=10 * 1000**3, bytes_accessed=8 * 1000**2, transcendentals=8 * 1000**2
        ),
        name="attention",
    )(x)


def pack_kernel(
    q_hbm, g_hbm, kv_hbm, seg_hbm, h_hbm, send_hbm, cols_hbm, seg_ref, h_ref, number_ref, cols_ref, sems
):
    tokens = q_hbm.shape[0]
    groups = HQ // HK
    dp, width = cols_ref.shape[0], cols_ref.shape[1]
    share = h_ref.shape[1] // (HQ * dp)
    rest = [
        pltpu.make_async_copy(seg_hbm, seg_ref, sems.at[4]),
        pltpu.make_async_copy(h_hbm, h_ref, sems.at[5]),
    ]
    for copy in rest:
        copy.start()
    copies = []
    for h in range(HQ):
        k = (h // groups) * DH
        sources = [(q_hbm, h * DH), (g_hbm, h * DH), (kv_hbm, k), (kv_hbm, HK * DH + k)]
        for slot, (source, first) in enumerate(sources):
            target = send_hbm.at[h, pl.ds(slot * tokens, tokens)]
            copies.append(
                pltpu.make_async_copy(source.at[:, pl.ds(first, DH)], target, sems.at[slot])
            )
    for copy in copies:
        copy.start()
    rest[0].wait()
    numbers = jnp.broadcast_to(seg_ref[...].astype(jnp.bfloat16), (SEGMENT_ROWS, tokens))
    for h in range(HQ):
        number_ref[h] = numbers
    rest.append(pltpu.make_async_copy(number_ref, send_hbm.at[:, 4 * tokens :], sems.at[6]))
    rest[2].start()
    rest[1].wait()
    span = share * dp
    for s in range(width // share):
        turned = h_ref[:, s * span : (s + 1) * span].T
        for r in range(dp):
            cols_ref[r, s * share : (s + 1) * share, :] = turned[r * share : (r + 1) * share]
    rest.append(pltpu.make_async_copy(cols_ref, cols_hbm, sems.at[7]))
    rest[3].start()
    for slot in range(4):
        whole = send_hbm.at[:, pl.ds(slot * tokens, tokens)]
        pltpu.make_async_copy(whole, whole, sems.at[slot]).wait()
    for copy in rest[2:]:
        copy.wait()


def combine_kernel(part_hbm, out_hbm, part_ref, out_ref, sems):
    groups = HQ // HK
    pieces = sems.shape[0] - 1
    some = HQ // pieces
    tokens = out_ref.shape[0]
    arrivals = []
    for j in range(pieces):
        at = pl.ds(j * some, some)
        arrivals.append(
            pltpu.make_async_copy(part_hbm.at[at, tokens:], part_ref.at[at], sems.at[j])
        )
    for copy in arrivals:
        copy.start()
    for g in range(HK):
        totals = [jnp.zeros((tokens, DH), jnp.float32)] * 2
        for h in range(g * groups, (g + 1) * groups):
            if h % some == 0:
                arrivals[h // some].wait()
            for kind in range(2):
                at = slice(kind * tokens, (kind + 1) * tokens)
                totals[kind] += part_ref[h, at, :].astype(jnp.float32)
        for kind in range(2):
            at = (kind * HK + g) * DH
            out_ref[:, at : at + DH] = totals[kind].astype(jnp.bfloat16)
    copy = pltpu.make_async_copy(out_ref, out_hbm, sems.at[pieces])
    copy.start()
    copy.wait()


def weight_kernel(cols_hbm, kv_hbm, out_hbm, cols_ref, kv_ref, out_ref, sems):
    parts, depth, _ = cols_ref.shape
    seq, share = out_ref.shape[0], out_ref.shape[1]
    rows, some = depth // parts, seq // parts
    first = pltpu.make_async_copy(kv_hbm, kv_ref, sems.at[2 * parts])
    first.start()
    arrivals, departures = [], []
    for j in range(parts):
        at, to = pl.ds(j * rows, rows), pl.ds(j * some, some)
        arrivals.append(
            pltpu.make_async_copy(cols_hbm.at[:, at], cols_ref.at[:, at], sems.at[j])
        )
        departures.append(
            pltpu.make_async_copy(out_ref.at[to], out_hbm.at[to], sems.at[parts + j])
        )
    for copy in arrivals:
        copy.start()
    first.wait()
    for j in range(parts):
        arrivals[j].wait()
        at = slice(j * rows, (j + 1) * rows)
        total = dot(cols_ref[0, at], kv_ref[0], NN)
        for r in range(1, parts):
            total += dot(cols_ref[r, at], kv_ref[r], NN)
        out_ref[j * some : (j + 1) * some] = total.astype(jnp.bfloat16).reshape(
            some, share, total.shape[1]
        )
        departures[j].start()
    for copy in departures:
        copy.wait()


def unpack_kernel(part_hbm, out_hbm, sem):
    tokens = out_hbm.shape[0]
    copies = []
    for h in range(HQ):
        target = out_hbm.at[:, pl.ds(h * DH, DH)]
        copies.append(pltpu.make_async_copy(part_hbm.at[h, pl.ds(0, tokens)], target, sem))
    for copy in copies:
        copy.start()
    pltpu.make_async_copy(out_hbm, out_hbm, sem).wait()


def total_kernel(part_hbm, out_hbm, part_ref, out_ref, sems):
    seq = part_ref.shape[0]
    pieces = sems.shape[0] - 1
    some = seq // pieces
    arrivals = []
    for j in range(pieces):
        at = pl.ds(j * some, some)
        arrivals.append(pltpu.make_async_copy(part_hbm.at[at], part_ref.at[at], sems.at[j]))
    for copy in arrivals:
        copy.start()
    total = jnp.zeros(out_ref.shape, jnp.float32)
    for j in range(pieces):
        arrivals[j].wait()
        for s in range(j * some, (j + 1) * some):
            total += part_ref[s].astype(jnp.float32)
    out_ref[...] = total
    copy = pltpu.make_async_copy(out_ref, out_hbm, sems.at[pieces])
    copy.start()
    copy.wait()


def exchange(array, axis):
    return lax.all_to_all(array, axis, split_axis=0, concat_axis=0, tiled=True)


def shards(hidden, queries, keyvals, out_grad, segment):
    seq, dp = lax.axis_size("seq"), lax.axis_size("dp")
    tokens, width = hidden.shape[1], hidden.shape[2]
    share = width // (seq * dp)
    half = jnp.bfloat16
    shape = jax.ShapeDtypeStruct

    inputs = [queries[0], out_grad[0], keyvals[0], segment, hidden[0]]
    send, columns = local(
        pack_kernel,
        (shape((HQ, 4 * tokens + SEGMENT_ROWS, DH), half), shape((dp, seq * share, tokens), half)),
        inputs,
        [
            pltpu.VMEM(segment.shape, segment.dtype),
            pltpu.VMEM(hidden.shape[1:], hidden.dtype),
            pltpu.VMEM((HQ, SEGMENT_ROWS, tokens), half),
            pltpu.VMEM((dp, seq * share, tokens), half),
            pltpu.SemaphoreType.DMA((8,)),
        ],
        "pack",
    )
    mine, columns = lax.optimization_barrier((exchange(send, "seq"), columns))
    columns = exchange(columns, "dp")
    grads, columns = lax.optimization_barrier((attention(mine), columns))
    back = exchange(grads, "seq")
    keyval_grad = local(
        combine_kernel,
        shape((tokens, 2 * HK * DH), half),
        [back],
        [
            pltpu.VMEM((HQ, 2 * tokens, DH), half),
            pltpu.VMEM((tokens, 2 * HK * DH), half),
            pltpu.SemaphoreType.DMA((9,)),
        ],
        "combine",
    )
    every = lax.all_gather(keyval_grad, "dp", axis=0)
    result = (seq, share, 2 * HK * DH)
    partial = local(
        weight_kernel,
        shape(result, half),
        [columns, every],
        [
            pltpu.VMEM(columns.shape, half),
            pltpu.VMEM(every.shape, half),
            pltpu.VMEM(result, half),
            pltpu.SemaphoreType.DMA((2 * dp + 1,)),
        ],
        "weight",
    )
    partial = exchange(partial, "seq")
    query_grad = local(
        unpack_kernel,
        shape((tokens, HQ * DH), half),
        [back],
        [pltpu.SemaphoreType.DMA],
        "unpack",
    )
    weight_grad = local(
        total_kernel,
        shape(result[1:], jnp.float32),
        [partial],
        [
            pltpu.VMEM(result, half),
            pltpu.VMEM(result[1:], jnp.float32),
            pltpu.SemaphoreType.DMA((5,)),
        ],
        "total",
    )
    return (query_grad[None], keyval_grad[None], weight_grad)


def solution(mesh):
    in_specs = (
        P("dp", "seq", None),
        P("dp", "seq", None),
        P("dp", "seq", None),
        P("dp", "seq", None),
        P("dp", "seq"),
    )
    out_specs = (P("dp", "seq", None), P("dp", "seq", None), P(("seq", "dp"), None))
    return jax.shard_map(shards, mesh=mesh, in_specs=in_specs, out_specs=out_specs, check_vma=False)
```

```python
import jax
import jax.numpy as jnp
from jax import lax
from jax.experimental import pallas as pl
from jax.experimental.pallas import tpu as pltpu
from jax.sharding import PartitionSpec as P

HQ = 32
HK = 2
DH = 128
SCALE = DH ** -0.5
EXP2_SCALE = SCALE * 1.4426950408889634
MASKED = -1e30
LOWEST = -1e29
SEGMENT_ROWS = 16
BQ = 512
UNIT = 512
CHUNKS = (4, 2, 1)
VMEM_LIMIT = 127 * 512 * 1024
NT = (((1,), (1,)), ((), ()))
NN = (((1,), (0,)), ((), ()))
TN = (((0,), (0,)), ((), ()))


def dot(a, b, dims):
    return lax.dot_general(a, b, dims, preferred_element_type=jnp.float32)


def attention_kernel(
    x_hbm, out_hbm, x_ref, out_ref, p_ref, dp_ref, m_ref, dk_ref, dv_ref, sems, out_sems
):
    blocks = x_ref.shape[0]
    seq = blocks * 128
    qn, un = BQ // 128, UNIT // 128
    steps = seq // BQ

    def arrival(i):
        at = pl.ds(i * qn, qn)
        return pltpu.make_async_copy(x_hbm.at[at, :512], x_ref.at[at, :512], sems.at[i])

    def departure(i):
        at = pl.ds(i * qn, qn)
        return pltpu.make_async_copy(
            out_ref.at[at, :128], out_hbm.at[at, :128], out_sems.at[i]
        )

    def final(i):
        at = pl.ds(i * qn, qn)
        return pltpu.make_async_copy(
            out_ref.at[at, 128:], out_hbm.at[at, 128:], out_sems.at[steps + i]
        )

    numbers = pltpu.make_async_copy(x_hbm.at[:, 512:], x_ref.at[:, 512:], sems.at[steps])
    numbers.start()
    for i in range(steps):
        arrival(i).start()
    dk_ref[...] = jnp.zeros_like(dk_ref)
    dv_ref[...] = jnp.zeros_like(dv_ref)
    numbers.wait()

    def rows(first, count, slot):
        part = x_ref[pl.ds(first, count), slot * 128 : (slot + 1) * 128, :]
        return part.reshape(count * 128, DH)

    segments = x_ref[:, 512:513, :].astype(jnp.float32)
    count0 = jnp.sum(jnp.where(segments < 0.5, 1.0, 0.0)).astype(jnp.int32)
    count1 = jnp.sum(jnp.where(segments < 1.5, 1.0, 0.0)).astype(jnp.int32)

    def start_of(pos):
        return jnp.where(pos >= count1, count1, jnp.where(pos >= count0, count0, 0))

    def query_block(i, _):
        arrival(i).wait()
        first = i * BQ
        q = rows(i * qn, qn, 0)
        cotan = rows(i * qn, qn, 1)
        qpos = first + lax.broadcasted_iota(jnp.int32, (1, BQ), 1)
        qstart = start_of(qpos)
        low = start_of(first) // UNIT
        high = (first + BQ - 1) // UNIT + 1

        def walk(body, state):
            at = low
            for size in CHUNKS:
                count = (high - at) // size

                def step(t, carry, size=size, at=at):
                    return body(at + t * size, size, carry)

                state = lax.fori_loop(0, count, step, state)
                at = at + count * size
            return state

        def scores(kb, size, carry):
            top, total, delta = carry
            k = rows(kb * un, size * un, 2)
            v = rows(kb * un, size * un, 3)
            st = dot(k, q, NT)
            dpt = dot(v, cotan, NT)
            at = pl.ds(pl.multiple_of(kb * UNIT, UNIT), size * UNIT)
            kpos = kb * UNIT + lax.broadcasted_iota(jnp.int32, (size * UNIT, BQ), 0)
            st = jnp.where((kpos >= qstart) & (kpos <= qpos), st, MASKED)
            newtop = jnp.maximum(top, jnp.max(st, axis=0, keepdims=True))
            p = jnp.exp2((st - newtop) * EXP2_SCALE)
            fade = jnp.exp2((top - newtop) * EXP2_SCALE)
            total = total * fade + jnp.sum(p, axis=0, keepdims=True)
            delta = delta * fade + jnp.sum(p * dpt, axis=0, keepdims=True)
            p_ref[at, :] = p
            dp_ref[at, :] = dpt
            m_ref[pl.ds(kb, 1), :] = newtop
            return newtop, total, delta

        zero = jnp.zeros((1, BQ), jnp.float32)
        top, total, delta = walk(scores, (zero + LOWEST, zero, zero))
        inverse = 1.0 / total
        delta = delta * inverse

        def grads(kb, size, dq):
            k = rows(kb * un, size * un, 2)
            at = pl.ds(pl.multiple_of(kb * UNIT, UNIT), size * UNIT)
            factor = jnp.exp2((m_ref[pl.ds(kb, 1), :] - top) * EXP2_SCALE) * inverse
            w = p_ref[at, :] * factor
            ds = (w * (dp_ref[at, :] - delta)).astype(jnp.bfloat16)
            dv_ref[at, :] += dot(w.astype(jnp.bfloat16), cotan, NN)
            dk_ref[at, :] += dot(ds, q, NN)
            return dq + dot(ds, k, TN)

        dq = walk(grads, jnp.zeros((BQ, DH), jnp.float32))
        out_ref[pl.ds(i * qn, qn), :128, :] = (
            (dq * SCALE).astype(jnp.bfloat16).reshape(qn, 128, DH)
        )
        departure(i).start()
        return 0

    lax.fori_loop(0, steps, query_block, 0)

    def finish(i, _):
        for b in range(qn):
            at = pl.ds(pl.multiple_of((i * qn + b) * 128, 128), 128)
            out_ref[i * qn + b, 128:256, :] = (dk_ref[at, :] * SCALE).astype(jnp.bfloat16)
            out_ref[i * qn + b, 256:384, :] = dv_ref[at, :].astype(jnp.bfloat16)
        final(i).start()
        return 0

    lax.fori_loop(0, steps, finish, 0)
    for i in range(steps):
        departure(i).wait()
        final(i).wait()


def local(body, out_shape, inputs, scratch, name):
    spec = pl.BlockSpec(memory_space=pltpu.HBM)
    many = isinstance(out_shape, tuple)
    return pl.pallas_call(
        body,
        out_shape=out_shape,
        in_specs=[spec] * len(inputs),
        out_specs=(spec,) * len(out_shape) if many else spec,
        scratch_shapes=scratch,
        compiler_params=pltpu.CompilerParams(vmem_limit_bytes=VMEM_LIMIT),
        name=name,
    )(*inputs)


def attention(x):
    blocks = x.shape[0]
    seq = blocks * 128
    return pl.pallas_call(
        attention_kernel,
        out_shape=jax.ShapeDtypeStruct((blocks, 384, DH), jnp.bfloat16),
        in_specs=[pl.BlockSpec(memory_space=pltpu.HBM)],
        out_specs=pl.BlockSpec(memory_space=pltpu.HBM),
        scratch_shapes=[
            pltpu.VMEM(x.shape, jnp.bfloat16),
            pltpu.VMEM((blocks, 384, DH), jnp.bfloat16),
            pltpu.VMEM((seq, BQ), jnp.float32),
            pltpu.VMEM((seq, BQ), jnp.float32),
            pltpu.VMEM((seq // UNIT, BQ), jnp.float32),
            pltpu.VMEM((seq, DH), jnp.float32),
            pltpu.VMEM((seq, DH), jnp.float32),
            pltpu.SemaphoreType.DMA((seq // BQ + 1,)),
            pltpu.SemaphoreType.DMA((2 * seq // BQ,)),
        ],
        compiler_params=pltpu.CompilerParams(vmem_limit_bytes=VMEM_LIMIT),
        cost_estimate=pl.CostEstimate(
            flops=10 * 1000**3, bytes_accessed=8 * 1000**2, transcendentals=8 * 1000**2
        ),
        name="attention",
    )(x)


def pack_kernel(
    q_hbm, g_hbm, kv_hbm, seg_hbm, h_hbm, send_hbm, cols_hbm, *scratch
):
    q_ref, g_ref, kv_ref, seg_ref, h_ref, send_ref, cols_ref, in_sems, out_sems = scratch
    pairs = [(seg_hbm, seg_ref), (kv_hbm, kv_ref), (q_hbm, q_ref), (g_hbm, g_ref), (h_hbm, h_ref)]
    arrivals = [pltpu.make_async_copy(*pair, in_sems.at[i]) for i, pair in enumerate(pairs)]
    for copy in arrivals:
        copy.start()
    tokens = q_ref.shape[0]
    groups = HQ // HK
    dp, width = cols_ref.shape[0], cols_ref.shape[1]
    share = h_ref.shape[1] // (HQ * dp)
    bounds = [(2 * tokens, 4 * tokens + SEGMENT_ROWS), (0, tokens), (tokens, 2 * tokens)]
    departures = []
    for i, (first, last) in enumerate(bounds):
        at = pl.ds(first, last - first)
        departures.append(
            pltpu.make_async_copy(send_ref.at[:, at], send_hbm.at[:, at], out_sems.at[i])
        )
    departures.append(pltpu.make_async_copy(cols_ref, cols_hbm, out_sems.at[3]))
    arrivals[0].wait()
    numbers = jnp.broadcast_to(seg_ref[...].astype(jnp.bfloat16), (SEGMENT_ROWS, tokens))
    arrivals[1].wait()
    for h in range(HQ):
        k = (h // groups) * DH
        v = HK * DH + k
        send_ref[h, 2 * tokens : 3 * tokens, :] = kv_ref[:, k : k + DH]
        send_ref[h, 3 * tokens : 4 * tokens, :] = kv_ref[:, v : v + DH]
        send_ref[h, 4 * tokens :, :] = numbers
    departures[0].start()
    for slot, ref in ((0, q_ref), (1, g_ref)):
        arrivals[2 + slot].wait()
        for h in range(HQ):
            send_ref[h, slot * tokens : (slot + 1) * tokens, :] = ref[:, h * DH : (h + 1) * DH]
        departures[1 + slot].start()
    arrivals[4].wait()
    span = share * dp
    for s in range(width // share):
        turned = h_ref[:, s * span : (s + 1) * span].T
        for r in range(dp):
            cols_ref[r, s * share : (s + 1) * share, :] = turned[r * share : (r + 1) * share]
    departures[3].start()
    for copy in departures:
        copy.wait()


def combine_kernel(part_hbm, out_hbm, part_ref, out_ref, sems):
    groups = HQ // HK
    pieces = sems.shape[0] - 1
    some = HQ // pieces
    tokens = out_ref.shape[0]
    arrivals = []
    for j in range(pieces):
        at = pl.ds(j * some, some)
        arrivals.append(
            pltpu.make_async_copy(part_hbm.at[at, tokens:], part_ref.at[at], sems.at[j])
        )
    for copy in arrivals:
        copy.start()
    for g in range(HK):
        totals = [jnp.zeros((tokens, DH), jnp.float32)] * 2
        for h in range(g * groups, (g + 1) * groups):
            if h % some == 0:
                arrivals[h // some].wait()
            for kind in range(2):
                at = slice(kind * tokens, (kind + 1) * tokens)
                totals[kind] += part_ref[h, at, :].astype(jnp.float32)
        for kind in range(2):
            at = (kind * HK + g) * DH
            out_ref[:, at : at + DH] = totals[kind].astype(jnp.bfloat16)
    copy = pltpu.make_async_copy(out_ref, out_hbm, sems.at[pieces])
    copy.start()
    copy.wait()


def weight_kernel(cols_hbm, kv_hbm, out_hbm, cols_ref, kv_ref, out_ref, sems):
    parts, depth, _ = cols_ref.shape
    seq, share = out_ref.shape[0], out_ref.shape[1]
    rows, some = depth // parts, seq // parts
    first = pltpu.make_async_copy(kv_hbm, kv_ref, sems.at[2 * parts])
    first.start()
    arrivals, departures = [], []
    for j in range(parts):
        at, to = pl.ds(j * rows, rows), pl.ds(j * some, some)
        arrivals.append(
            pltpu.make_async_copy(cols_hbm.at[:, at], cols_ref.at[:, at], sems.at[j])
        )
        departures.append(
            pltpu.make_async_copy(out_ref.at[to], out_hbm.at[to], sems.at[parts + j])
        )
    for copy in arrivals:
        copy.start()
    first.wait()
    for j in range(parts):
        arrivals[j].wait()
        at = slice(j * rows, (j + 1) * rows)
        total = dot(cols_ref[0, at], kv_ref[0], NN)
        for r in range(1, parts):
            total += dot(cols_ref[r, at], kv_ref[r], NN)
        out_ref[j * some : (j + 1) * some] = total.astype(jnp.bfloat16).reshape(
            some, share, total.shape[1]
        )
        departures[j].start()
    for copy in departures:
        copy.wait()


def unpack_kernel(part_hbm, out_hbm, part_ref, out_ref, sems):
    tokens = out_ref.shape[0]
    copy = pltpu.make_async_copy(part_hbm.at[:, :tokens], part_ref, sems.at[0])
    copy.start()
    copy.wait()
    for h in range(HQ):
        out_ref[:, h * DH : (h + 1) * DH] = part_ref[h]
    copy = pltpu.make_async_copy(out_ref, out_hbm, sems.at[1])
    copy.start()
    copy.wait()


def total_kernel(part_hbm, out_hbm, part_ref, out_ref, sems):
    seq = part_ref.shape[0]
    pieces = sems.shape[0] - 1
    some = seq // pieces
    arrivals = []
    for j in range(pieces):
        at = pl.ds(j * some, some)
        arrivals.append(pltpu.make_async_copy(part_hbm.at[at], part_ref.at[at], sems.at[j]))
    for copy in arrivals:
        copy.start()
    total = jnp.zeros(out_ref.shape, jnp.float32)
    for j in range(pieces):
        arrivals[j].wait()
        for s in range(j * some, (j + 1) * some):
            total += part_ref[s].astype(jnp.float32)
    out_ref[...] = total
    copy = pltpu.make_async_copy(out_ref, out_hbm, sems.at[pieces])
    copy.start()
    copy.wait()


def exchange(array, axis):
    return lax.all_to_all(array, axis, split_axis=0, concat_axis=0, tiled=True)


def shards(hidden, queries, keyvals, out_grad, segment):
    seq, dp = lax.axis_size("seq"), lax.axis_size("dp")
    tokens, width = hidden.shape[1], hidden.shape[2]
    share = width // (seq * dp)
    half = jnp.bfloat16
    shape = jax.ShapeDtypeStruct

    inputs = [queries[0], out_grad[0], keyvals[0], segment, hidden[0]]
    send, columns = local(
        pack_kernel,
        (shape((HQ, 4 * tokens + SEGMENT_ROWS, DH), half), shape((dp, seq * share, tokens), half)),
        inputs,
        [
            pltpu.VMEM(queries.shape[1:], half),
            pltpu.VMEM(out_grad.shape[1:], half),
            pltpu.VMEM(keyvals.shape[1:], half),
            pltpu.VMEM(segment.shape, segment.dtype),
            pltpu.VMEM(hidden.shape[1:], half),
            pltpu.VMEM((HQ, 4 * tokens + SEGMENT_ROWS, DH), half),
            pltpu.VMEM((dp, seq * share, tokens), half),
            pltpu.SemaphoreType.DMA((5,)),
            pltpu.SemaphoreType.DMA((4,)),
        ],
        "pack",
    )
    mine, columns = lax.optimization_barrier((exchange(send, "seq"), columns))
    columns = exchange(columns, "dp")
    grads, columns = lax.optimization_barrier((attention(mine), columns))
    back = exchange(grads, "seq")
    keyval_grad = local(
        combine_kernel,
        shape((tokens, 2 * HK * DH), half),
        [back],
        [
            pltpu.VMEM((HQ, 2 * tokens, DH), half),
            pltpu.VMEM((tokens, 2 * HK * DH), half),
            pltpu.SemaphoreType.DMA((9,)),
        ],
        "combine",
    )
    every = lax.all_gather(keyval_grad, "dp", axis=0)
    result = (seq, share, 2 * HK * DH)
    partial = local(
        weight_kernel,
        shape(result, half),
        [columns, every],
        [
            pltpu.VMEM(columns.shape, half),
            pltpu.VMEM(every.shape, half),
            pltpu.VMEM(result, half),
            pltpu.SemaphoreType.DMA((2 * dp + 1,)),
        ],
        "weight",
    )
    partial = exchange(partial, "seq")
    query_grad = local(
        unpack_kernel,
        shape((tokens, HQ * DH), half),
        [back],
        [
            pltpu.VMEM((HQ, tokens, DH), half),
            pltpu.VMEM((tokens, HQ * DH), half),
            pltpu.SemaphoreType.DMA((2,)),
        ],
        "unpack",
    )
    weight_grad = local(
        total_kernel,
        shape(result[1:], jnp.float32),
        [partial],
        [
            pltpu.VMEM(result, half),
            pltpu.VMEM(result[1:], jnp.float32),
            pltpu.SemaphoreType.DMA((5,)),
        ],
        "total",
    )
    return (query_grad[None], keyval_grad[None], weight_grad)


def solution(mesh):
    in_specs = (
        P("dp", "seq", None),
        P("dp", "seq", None),
        P("dp", "seq", None),
        P("dp", "seq", None),
        P("dp", "seq"),
    )
    out_specs = (P("dp", "seq", None), P("dp", "seq", None), P(("seq", "dp"), None))
    return jax.shard_map(shards, mesh=mesh, in_specs=in_specs, out_specs=out_specs, check_vma=False)
```

```python
import jax
import jax.numpy as jnp
from jax import lax
from jax.experimental import pallas as pl
from jax.experimental.pallas import tpu as pltpu
from jax.sharding import PartitionSpec as P

HQ = 32
HK = 2
DH = 128
SCALE = DH ** -0.5
EXP2_SCALE = SCALE * 1.4426950408889634
MASKED = -1e30
LOWEST = -1e29
SEGMENT_ROWS = 16
BQ = 512
UNIT = 256
CHUNKS = (4, 2, 1)
VMEM_LIMIT = 127 * 512 * 1024
SMALL_LIMIT = 20 * 1024 * 1024
NT = (((1,), (1,)), ((), ()))
NN = (((1,), (0,)), ((), ()))


def dot(a, b, dims):
    return lax.dot_general(a, b, dims, preferred_element_type=jnp.float32)


def attention_kernel(
    x_hbm, out_hbm, x_ref, out_ref, p_ref, dp_ref, m_ref, dk_ref, dv_ref, kt_ref, sems, out_sems
):
    blocks = x_ref.shape[0]
    seq = blocks * 128
    qn, un = BQ // 128, UNIT // 128
    steps = seq // BQ

    def arrival(i):
        at = pl.ds(i * qn, qn)
        return pltpu.make_async_copy(x_hbm.at[at, :512], x_ref.at[at, :512], sems.at[i])

    def departure(i):
        at = pl.ds(i * qn, qn)
        return pltpu.make_async_copy(
            out_ref.at[at, :128], out_hbm.at[at, :128], out_sems.at[i]
        )

    def final(i):
        at = pl.ds(i * qn, qn)
        return pltpu.make_async_copy(
            out_ref.at[at, 128:], out_hbm.at[at, 128:], out_sems.at[steps + i]
        )

    numbers = pltpu.make_async_copy(x_hbm.at[:, 512:], x_ref.at[:, 512:], sems.at[steps])
    numbers.start()
    for i in range(steps):
        arrival(i).start()
    dk_ref[...] = jnp.zeros_like(dk_ref)
    dv_ref[...] = jnp.zeros_like(dv_ref)
    numbers.wait()

    def rows(first, count, slot):
        part = x_ref[pl.ds(first, count), slot * 128 : (slot + 1) * 128, :]
        return part.reshape(count * 128, DH)

    segments = x_ref[:, 512:513, :].astype(jnp.float32)
    count0 = jnp.sum(jnp.where(segments < 0.5, 1.0, 0.0)).astype(jnp.int32)
    count1 = jnp.sum(jnp.where(segments < 1.5, 1.0, 0.0)).astype(jnp.int32)

    def start_of(pos):
        return jnp.where(pos >= count1, count1, jnp.where(pos >= count0, count0, 0))

    def query_block(i, _):
        arrival(i).wait()
        first = i * BQ
        q = rows(i * qn, qn, 0)
        cotan = rows(i * qn, qn, 1)
        for b in range(qn):
            at = pl.ds(pl.multiple_of(first + b * 128, 128), 128)
            kt_ref[:, at] = x_ref[i * qn + b, 256:384, :].T
        qpos = first + lax.broadcasted_iota(jnp.int32, (1, BQ), 1)
        qstart = start_of(qpos)
        low = start_of(first) // UNIT
        high = (first + BQ - 1) // UNIT + 1

        def walk(body, state):
            at = low
            for size in CHUNKS:
                count = (high - at) // size

                def step(t, carry, size=size, at=at):
                    return body(at + t * size, size, carry)

                state = lax.fori_loop(0, count, step, state)
                at = at + count * size
            return state

        def scores(kb, size, carry):
            top, total, delta = carry
            k = rows(kb * un, size * un, 2)
            v = rows(kb * un, size * un, 3)
            st = dot(k, q, NT)
            dpt = dot(v, cotan, NT)
            at = pl.ds(pl.multiple_of(kb * UNIT, UNIT), size * UNIT)
            kpos = kb * UNIT + lax.broadcasted_iota(jnp.int32, (size * UNIT, BQ), 0)
            st = jnp.where((kpos >= qstart) & (kpos <= qpos), st, MASKED)
            newtop = jnp.maximum(top, jnp.max(st, axis=0, keepdims=True))
            p = jnp.exp2((st - newtop) * EXP2_SCALE)
            fade = jnp.exp2((top - newtop) * EXP2_SCALE)
            total = total * fade + jnp.sum(p, axis=0, keepdims=True)
            delta = delta * fade + jnp.sum(p * dpt, axis=0, keepdims=True)
            p_ref[at, :] = p
            dp_ref[at, :] = dpt
            m_ref[pl.ds(kb, 1), :] = newtop
            return newtop, total, delta

        zero = jnp.zeros((1, BQ), jnp.float32)
        top, total, delta = walk(scores, (zero + LOWEST, zero, zero))
        inverse = 1.0 / total
        delta = delta * inverse

        def grads(kb, size, dq):
            at = pl.ds(pl.multiple_of(kb * UNIT, UNIT), size * UNIT)
            factor = jnp.exp2((m_ref[pl.ds(kb, 1), :] - top) * EXP2_SCALE) * inverse
            w = p_ref[at, :] * factor
            ds = (w * (dp_ref[at, :] - delta)).astype(jnp.bfloat16)
            dv_ref[at, :] += dot(w.astype(jnp.bfloat16), cotan, NN)
            dk_ref[at, :] += dot(ds, q, NN)
            return dq + dot(kt_ref[:, at], ds, NN)

        dq = walk(grads, jnp.zeros((DH, BQ), jnp.float32)).T
        out_ref[pl.ds(i * qn, qn), :128, :] = (
            (dq * SCALE).astype(jnp.bfloat16).reshape(qn, 128, DH)
        )
        departure(i).start()
        return 0

    lax.fori_loop(0, steps, query_block, 0)

    def finish(i, _):
        for b in range(qn):
            at = pl.ds(pl.multiple_of((i * qn + b) * 128, 128), 128)
            out_ref[i * qn + b, 128:256, :] = (dk_ref[at, :] * SCALE).astype(jnp.bfloat16)
            out_ref[i * qn + b, 256:384, :] = dv_ref[at, :].astype(jnp.bfloat16)
        final(i).start()
        return 0

    lax.fori_loop(0, steps, finish, 0)
    for i in range(steps):
        departure(i).wait()
        final(i).wait()


def local(body, out_shape, inputs, scratch, name):
    spec = pl.BlockSpec(memory_space=pltpu.HBM)
    many = isinstance(out_shape, tuple)
    return pl.pallas_call(
        body,
        out_shape=out_shape,
        in_specs=[spec] * len(inputs),
        out_specs=(spec,) * len(out_shape) if many else spec,
        scratch_shapes=scratch,
        compiler_params=pltpu.CompilerParams(vmem_limit_bytes=VMEM_LIMIT),
        name=name,
    )(*inputs)


def attention(x):
    blocks = x.shape[0]
    seq = blocks * 128
    return pl.pallas_call(
        attention_kernel,
        out_shape=jax.ShapeDtypeStruct((blocks, 384, DH), jnp.bfloat16),
        in_specs=[pl.BlockSpec(memory_space=pltpu.HBM)],
        out_specs=pl.BlockSpec(memory_space=pltpu.HBM),
        scratch_shapes=[
            pltpu.VMEM(x.shape, jnp.bfloat16),
            pltpu.VMEM((blocks, 384, DH), jnp.bfloat16),
            pltpu.VMEM((seq, BQ), jnp.float32),
            pltpu.VMEM((seq, BQ), jnp.float32),
            pltpu.VMEM((seq // UNIT, BQ), jnp.float32),
            pltpu.VMEM((seq, DH), jnp.float32),
            pltpu.VMEM((seq, DH), jnp.float32),
            pltpu.VMEM((DH, seq), jnp.bfloat16),
            pltpu.SemaphoreType.DMA((seq // BQ + 1,)),
            pltpu.SemaphoreType.DMA((2 * seq // BQ,)),
        ],
        compiler_params=pltpu.CompilerParams(vmem_limit_bytes=VMEM_LIMIT),
        cost_estimate=pl.CostEstimate(
            flops=10 * 1000**3, bytes_accessed=8 * 1000**2, transcendentals=8 * 1000**2
        ),
        name="attention",
    )(x)


def pack_kernel(q_hbm, g_hbm, kv_hbm, seg_hbm, h_hbm, send_hbm, *rest):
    cols_hbm, scratch = rest[:-9], rest[-9:]
    mine = lax.axis_index("dp")
    q_ref, g_ref, kv_ref, seg_ref, h_ref, send_ref, cols_ref, in_sems, out_sems = scratch
    pairs = [(seg_hbm, seg_ref), (kv_hbm, kv_ref), (q_hbm, q_ref), (g_hbm, g_ref), (h_hbm, h_ref)]
    arrivals = [pltpu.make_async_copy(*pair, in_sems.at[i]) for i, pair in enumerate(pairs)]
    for copy in arrivals:
        copy.start()
    tokens = q_ref.shape[0]
    groups = HQ // HK
    dp, width = cols_ref.shape[0], cols_ref.shape[1]
    share = h_ref.shape[1] // (HQ * dp)
    bounds = [(2 * tokens, 4 * tokens + SEGMENT_ROWS), (0, tokens), (tokens, 2 * tokens)]
    departures = []
    for i, (first, last) in enumerate(bounds):
        at = pl.ds(first, last - first)
        departures.append(
            pltpu.make_async_copy(send_ref.at[:, at], send_hbm.at[:, at], out_sems.at[i])
        )
    for k, target in enumerate(cols_hbm):
        departures.append(pltpu.make_async_copy(cols_ref.at[k], target, out_sems.at[3 + k]))
    arrivals[0].wait()
    numbers = jnp.broadcast_to(seg_ref[...].astype(jnp.bfloat16), (SEGMENT_ROWS, tokens))
    arrivals[1].wait()
    for h in range(HQ):
        k = (h // groups) * DH
        v = HK * DH + k
        send_ref[h, 2 * tokens : 3 * tokens, :] = kv_ref[:, k : k + DH]
        send_ref[h, 3 * tokens : 4 * tokens, :] = kv_ref[:, v : v + DH]
        send_ref[h, 4 * tokens :, :] = numbers
    departures[0].start()
    for slot, ref in ((0, q_ref), (1, g_ref)):
        arrivals[2 + slot].wait()
        for h in range(HQ):
            send_ref[h, slot * tokens : (slot + 1) * tokens, :] = ref[:, h * DH : (h + 1) * DH]
        departures[1 + slot].start()
    arrivals[4].wait()
    span = share * dp
    for s in range(width // share):
        turned = h_ref[:, s * span : (s + 1) * span].T
        for r in range(dp):
            part = turned[r * share : (r + 1) * share]
            cols_ref[jnp.bitwise_xor(mine, r), s * share : (s + 1) * share, :] = part
    for copy in departures[3:]:
        copy.start()
    for copy in departures:
        copy.wait()


def combine_kernel(part_hbm, out_hbm, part_ref, out_ref, sems):
    groups = HQ // HK
    pieces = sems.shape[0] - 1
    some = HQ // pieces
    tokens = out_ref.shape[0]
    arrivals = []
    for j in range(pieces):
        at = pl.ds(j * some, some)
        arrivals.append(
            pltpu.make_async_copy(part_hbm.at[at, tokens:], part_ref.at[at], sems.at[j])
        )
    for copy in arrivals:
        copy.start()
    for g in range(HK):
        totals = [jnp.zeros((tokens, DH), jnp.float32)] * 2
        for h in range(g * groups, (g + 1) * groups):
            if h % some == 0:
                arrivals[h // some].wait()
            for kind in range(2):
                at = slice(kind * tokens, (kind + 1) * tokens)
                totals[kind] += part_ref[h, at, :].astype(jnp.float32)
        for kind in range(2):
            at = (kind * HK + g) * DH
            out_ref[:, at : at + DH] = totals[kind].astype(jnp.bfloat16)
    copy = pltpu.make_async_copy(out_ref, out_hbm, sems.at[pieces])
    copy.start()
    copy.wait()


def weight_kernel(*refs):
    *cols_ref, kv_ref, out_hbm, out_ref, sems = refs
    mine = lax.axis_index("dp")
    seq, share = out_ref.shape[0], out_ref.shape[1]
    pieces = sems.shape[0]
    some = seq // pieces
    departures = []
    for j in range(pieces):
        to = pl.ds(j * some, some)
        departures.append(
            pltpu.make_async_copy(out_ref.at[to], out_hbm.at[to], sems.at[j])
        )
        at = slice(j * some * share, (j + 1) * some * share)
        total = dot(cols_ref[0][at], kv_ref[mine], NN)
        for r in range(1, len(cols_ref)):
            total += dot(cols_ref[r][at], kv_ref[jnp.bitwise_xor(mine, r)], NN)
        out_ref[j * some : (j + 1) * some] = total.astype(jnp.bfloat16).reshape(
            some, share, total.shape[1]
        )
        departures[j].start()
    for copy in departures:
        copy.wait()


def unpack_kernel(part_hbm, out_hbm, part_ref, out_ref, sems):
    tokens = out_ref.shape[0]
    copy = pltpu.make_async_copy(part_hbm.at[:, :tokens], part_ref, sems.at[0])
    copy.start()
    copy.wait()
    for h in range(HQ):
        out_ref[:, h * DH : (h + 1) * DH] = part_ref[h]
    copy = pltpu.make_async_copy(out_ref, out_hbm, sems.at[1])
    copy.start()
    copy.wait()


def total_kernel(part_hbm, out_hbm, part_ref, out_ref, sems):
    seq = part_ref.shape[0]
    pieces = sems.shape[0] - 1
    some = seq // pieces
    arrivals = []
    for j in range(pieces):
        at = pl.ds(j * some, some)
        arrivals.append(pltpu.make_async_copy(part_hbm.at[at], part_ref.at[at], sems.at[j]))
    for copy in arrivals:
        copy.start()
    total = jnp.zeros(out_ref.shape, jnp.float32)
    for j in range(pieces):
        arrivals[j].wait()
        for s in range(j * some, (j + 1) * some):
            total += part_ref[s].astype(jnp.float32)
    out_ref[...] = total
    copy = pltpu.make_async_copy(out_ref, out_hbm, sems.at[pieces])
    copy.start()
    copy.wait()


def exchange(array, axis):
    return lax.all_to_all(array, axis, split_axis=0, concat_axis=0, tiled=True)


def shards(hidden, queries, keyvals, out_grad, segment):
    seq, dp = lax.axis_size("seq"), lax.axis_size("dp")
    tokens, width = hidden.shape[1], hidden.shape[2]
    share = width // (seq * dp)
    half = jnp.bfloat16
    shape = jax.ShapeDtypeStruct

    inputs = [queries[0], out_grad[0], keyvals[0], segment, hidden[0]]
    column = shape((seq * share, tokens), half)
    send, *columns = local(
        pack_kernel,
        (shape((HQ, 4 * tokens + SEGMENT_ROWS, DH), half),) + (column,) * dp,
        inputs,
        [
            pltpu.VMEM(queries.shape[1:], half),
            pltpu.VMEM(out_grad.shape[1:], half),
            pltpu.VMEM(keyvals.shape[1:], half),
            pltpu.VMEM(segment.shape, segment.dtype),
            pltpu.VMEM(hidden.shape[1:], half),
            pltpu.VMEM((HQ, 4 * tokens + SEGMENT_ROWS, DH), half),
            pltpu.VMEM((dp, seq * share, tokens), half),
            pltpu.SemaphoreType.DMA((5,)),
            pltpu.SemaphoreType.DMA((3 + dp,)),
        ],
        "pack",
    )
    mine, columns = lax.optimization_barrier((exchange(send, "seq"), columns))
    for k in range(1, dp):
        columns[k] = lax.ppermute(columns[k], "dp", [(r, r ^ k) for r in range(dp)])
    grads, columns = lax.optimization_barrier((attention(mine), columns))
    back = exchange(grads, "seq")
    keyval_grad = local(
        combine_kernel,
        shape((tokens, 2 * HK * DH), half),
        [back],
        [
            pltpu.VMEM((HQ, 2 * tokens, DH), half),
            pltpu.VMEM((tokens, 2 * HK * DH), half),
            pltpu.SemaphoreType.DMA((9,)),
        ],
        "combine",
    )
    every = lax.all_gather(keyval_grad, "dp", axis=0)
    result = (seq, share, 2 * HK * DH)
    partial = pl.pallas_call(
        weight_kernel,
        out_shape=shape(result, half),
        in_specs=[pl.BlockSpec(memory_space=pltpu.VMEM)] * (dp + 1),
        out_specs=pl.BlockSpec(memory_space=pltpu.HBM),
        scratch_shapes=[pltpu.VMEM(result, half), pltpu.SemaphoreType.DMA((4,))],
        compiler_params=pltpu.CompilerParams(vmem_limit_bytes=SMALL_LIMIT),
        name="weight",
    )(*columns, every)
    partial = exchange(partial, "seq")
    query_grad = local(
        unpack_kernel,
        shape((tokens, HQ * DH), half),
        [back],
        [
            pltpu.VMEM((HQ, tokens, DH), half),
            pltpu.VMEM((tokens, HQ * DH), half),
            pltpu.SemaphoreType.DMA((2,)),
        ],
        "unpack",
    )
    weight_grad = local(
        total_kernel,
        shape(result[1:], jnp.float32),
        [partial],
        [
            pltpu.VMEM(result, half),
            pltpu.VMEM(result[1:], jnp.float32),
            pltpu.SemaphoreType.DMA((5,)),
        ],
        "total",
    )
    return (query_grad[None], keyval_grad[None], weight_grad)


def solution(mesh):
    in_specs = (
        P("dp", "seq", None),
        P("dp", "seq", None),
        P("dp", "seq", None),
        P("dp", "seq", None),
        P("dp", "seq"),
    )
    out_specs = (P("dp", "seq", None), P("dp", "seq", None), P(("seq", "dp"), None))
    return jax.shard_map(shards, mesh=mesh, in_specs=in_specs, out_specs=out_specs, check_vma=False)
```

```python
import jax
import jax.numpy as jnp
from jax import lax
from jax.experimental import pallas as pl
from jax.experimental.pallas import tpu as pltpu
from jax.sharding import PartitionSpec as P

HQ = 32
HK = 2
DH = 128
SCALE = DH ** -0.5
EXP2_SCALE = SCALE * 1.4426950408889634
MASKED = -1e30
LOWEST = -1e29
SEGMENT_ROWS = 16
BQ = 512
UNIT = 256
CHUNKS = (8, 4, 2, 1)
PLANES = 8
VMEM_LIMIT = 127 * 512 * 1024
SMALL_LIMIT = 20 * 1024 * 1024
NT = (((1,), (1,)), ((), ()))
NN = (((1,), (0,)), ((), ()))


def dot(a, b, dims):
    return lax.dot_general(a, b, dims, preferred_element_type=jnp.float32)


def attention_kernel(*refs):
    kv_hbm, q_hbm = refs[0], refs[1:5]
    dkv_hbm, dq_hbm = refs[5], refs[6:10]
    x_ref, seg_ref, q_ref, dq_ref, dkv_ref = refs[10:15]
    p_ref, dp_ref, m_ref, dk_ref, dv_ref, kt_ref, sems, out_sems = refs[15:]
    planes, lines = kv_hbm.shape[0], kv_hbm.shape[1]
    blocks = planes * lines
    seq = blocks * 128
    un = UNIT // 128
    mine = lax.axis_index("seq")
    line, plane = mine // planes, mine % planes

    arrivals = []
    for j in range(lines):
        at = pl.ds(j * planes, planes)
        arrivals.append(
            pltpu.make_async_copy(kv_hbm.at[:, j, 256:], seg_ref.at[at], sems.at[j])
        )
    for j in range(lines):
        at = pl.ds(j * planes, planes)
        arrivals.append(
            pltpu.make_async_copy(kv_hbm.at[:, j, :256], x_ref.at[at], sems.at[lines + j])
        )
    for j in range(lines):
        arrivals.append(pltpu.make_async_copy(q_hbm[j], q_ref.at[j], sems.at[2 * lines + j]))
    for copy in arrivals:
        copy.start()

    def departure(j):
        return pltpu.make_async_copy(dq_ref.at[j], dq_hbm[j], out_sems.at[j])

    def final(j):
        return pltpu.make_async_copy(dkv_ref.at[:, j], dkv_hbm.at[:, j], out_sems.at[lines + j])

    dk_ref[...] = jnp.zeros_like(dk_ref)
    dv_ref[...] = jnp.zeros_like(dv_ref)
    for copy in arrivals:
        copy.wait()

    def rows(first, count, slot):
        part = x_ref[pl.ds(first, count), slot * 128 : (slot + 1) * 128, :]
        return part.reshape(count * 128, DH)

    def turn(b, _):
        kt_ref[:, pl.ds(pl.multiple_of(b * 128, 128), 128)] = x_ref[b, :128, :].T
        return 0

    lax.fori_loop(0, blocks, turn, 0)
    segments = seg_ref[:, 0:1, :].astype(jnp.float32)
    count0 = jnp.sum(jnp.where(segments < 0.5, 1.0, 0.0)).astype(jnp.int32)
    count1 = jnp.sum(jnp.where(segments < 1.5, 1.0, 0.0)).astype(jnp.int32)

    def start_of(pos):
        return jnp.where(pos >= count1, count1, jnp.where(pos >= count0, count0, 0))

    heads = dq_ref.shape[1]
    some = BQ // 128
    turns = heads // some

    def query_block(i, _):
        j, part = i // turns, i % turns
        first = (jnp.bitwise_xor(line, j) * planes + plane) * 128
        q = q_ref[j, pl.ds(part * some, some)].reshape(BQ, DH)
        cotan = q_ref[j, pl.ds(heads + part * some, some)].reshape(BQ, DH)
        qpos = first + lax.broadcasted_iota(jnp.int32, (1, BQ), 1) % 128
        qstart = start_of(qpos)
        low = start_of(first) // UNIT
        high = (first + 127) // UNIT + 1

        def walk(body, state):
            at = low
            for size in CHUNKS:
                count = (high - at) // size

                def step(t, carry, size=size, at=at):
                    return body(at + t * size, size, carry)

                state = lax.fori_loop(0, count, step, state)
                at = at + count * size
            return state

        def scores(kb, size, carry):
            top, total, delta = carry
            k = rows(kb * un, size * un, 0)
            v = rows(kb * un, size * un, 1)
            st = dot(k, q, NT)
            dpt = dot(v, cotan, NT)
            at = pl.ds(pl.multiple_of(kb * UNIT, UNIT), size * UNIT)
            kpos = kb * UNIT + lax.broadcasted_iota(jnp.int32, (size * UNIT, BQ), 0)
            st = jnp.where((kpos >= qstart) & (kpos <= qpos), st, MASKED)
            newtop = jnp.maximum(top, jnp.max(st, axis=0, keepdims=True))
            p = jnp.exp2((st - newtop) * EXP2_SCALE)
            fade = jnp.exp2((top - newtop) * EXP2_SCALE)
            total = total * fade + jnp.sum(p, axis=0, keepdims=True)
            delta = delta * fade + jnp.sum(p * dpt, axis=0, keepdims=True)
            p_ref[at, :] = p
            dp_ref[at, :] = dpt
            m_ref[pl.ds(kb, 1), :] = newtop
            return newtop, total, delta

        zero = jnp.zeros((1, BQ), jnp.float32)
        top, total, delta = walk(scores, (zero + LOWEST, zero, zero))
        inverse = 1.0 / total
        delta = delta * inverse

        def grads(kb, size, dq):
            at = pl.ds(pl.multiple_of(kb * UNIT, UNIT), size * UNIT)
            factor = jnp.exp2((m_ref[pl.ds(kb, 1), :] - top) * EXP2_SCALE) * inverse
            w = p_ref[at, :] * factor
            ds = (w * (dp_ref[at, :] - delta)).astype(jnp.bfloat16)
            dv_ref[at, :] += dot(w.astype(jnp.bfloat16), cotan, NN)
            dk_ref[at, :] += dot(ds, q, NN)
            return dq + dot(kt_ref[:, at], ds, NN)

        dq = walk(grads, jnp.zeros((DH, BQ), jnp.float32)).T
        dq_ref[j, pl.ds(part * some, some)] = (
            (dq * SCALE).astype(jnp.bfloat16).reshape(some, 128, DH)
        )
        for k in range(lines):
            pl.when(i == (k + 1) * turns - 1)(departure(k).start)
        return 0

    lax.fori_loop(0, lines * turns, query_block, 0)

    def finish(b, _):
        at = pl.ds(pl.multiple_of(b * 128, 128), 128)
        dkv_ref[b % planes, b // planes, :128, :] = (dk_ref[at, :] * SCALE).astype(jnp.bfloat16)
        dkv_ref[b % planes, b // planes, 128:, :] = dv_ref[at, :].astype(jnp.bfloat16)
        return 0

    for j in range(lines):
        lax.fori_loop(j * planes, (j + 1) * planes, finish, 0)
        final(j).start()
    for j in range(lines):
        departure(j).wait()
        final(j).wait()


def local(body, out_shape, inputs, scratch, name):
    spec = pl.BlockSpec(memory_space=pltpu.HBM)
    many = isinstance(out_shape, tuple)
    return pl.pallas_call(
        body,
        out_shape=out_shape,
        in_specs=[spec] * len(inputs),
        out_specs=(spec,) * len(out_shape) if many else spec,
        scratch_shapes=scratch,
        compiler_params=pltpu.CompilerParams(vmem_limit_bytes=VMEM_LIMIT),
        name=name,
    )(*inputs)


def attention(kv, parts):
    planes, lines = kv.shape[0], kv.shape[1]
    blocks = planes * lines
    seq = blocks * 128
    heads = parts[0].shape[0] // 2
    half = jnp.bfloat16
    shape = jax.ShapeDtypeStruct
    spec = pl.BlockSpec(memory_space=pltpu.HBM)
    return pl.pallas_call(
        attention_kernel,
        out_shape=(shape((planes, lines, 256, DH), half),)
        + (shape((heads, 128, DH), half),) * lines,
        in_specs=[spec] * (1 + lines),
        out_specs=(spec,) * (1 + lines),
        scratch_shapes=[
            pltpu.VMEM((blocks, 256, DH), half),
            pltpu.VMEM((blocks, SEGMENT_ROWS, 128), half),
            pltpu.VMEM((lines, 2 * heads, 128, DH), half),
            pltpu.VMEM((lines, heads, 128, DH), half),
            pltpu.VMEM((planes, lines, 256, DH), half),
            pltpu.VMEM((seq, BQ), jnp.float32),
            pltpu.VMEM((seq, BQ), jnp.float32),
            pltpu.VMEM((max(8, seq // UNIT), BQ), jnp.float32),
            pltpu.VMEM((seq, DH), jnp.float32),
            pltpu.VMEM((seq, DH), jnp.float32),
            pltpu.VMEM((DH, seq), half),
            pltpu.SemaphoreType.DMA((3 * lines,)),
            pltpu.SemaphoreType.DMA((2 * lines,)),
        ],
        compiler_params=pltpu.CompilerParams(vmem_limit_bytes=VMEM_LIMIT),
        cost_estimate=pl.CostEstimate(
            flops=10 * 1000**3, bytes_accessed=8 * 1000**2, transcendentals=8 * 1000**2
        ),
        name="attention",
    )(kv, *parts)


def pack_kernel(q_hbm, g_hbm, kv_hbm, seg_hbm, h_hbm, *rest):
    kv_out, q_out, cols_out = rest[0], rest[1:5], rest[5:9]
    q_ref, g_ref, kv_ref, seg_ref, h_ref, kv_send, q_send, cols_ref, in_sems, out_sems = rest[9:]
    line, core = lax.axis_index("seq") // PLANES, lax.axis_index("dp")
    pairs = [(seg_hbm, seg_ref), (kv_hbm, kv_ref), (q_hbm, q_ref), (g_hbm, g_ref), (h_hbm, h_ref)]
    arrivals = [pltpu.make_async_copy(*pair, in_sems.at[i]) for i, pair in enumerate(pairs)]
    for copy in arrivals:
        copy.start()
    tokens = q_ref.shape[0]
    lines, heads = q_send.shape[0], q_send.shape[1] // 2
    dp, width = cols_ref.shape[0], cols_ref.shape[1]
    share = h_ref.shape[1] // (HQ * dp)
    departures = [pltpu.make_async_copy(kv_send, kv_out, out_sems.at[0])]
    for k in range(lines):
        departures.append(pltpu.make_async_copy(q_send.at[k], q_out[k], out_sems.at[1 + k]))
    for k in range(dp):
        sem = out_sems.at[1 + lines + k]
        departures.append(pltpu.make_async_copy(cols_ref.at[k], cols_out[k], sem))
    arrivals[0].wait()
    numbers = jnp.broadcast_to(seg_ref[...].astype(jnp.bfloat16), (SEGMENT_ROWS, tokens))
    arrivals[1].wait()
    for j in range(lines):
        k = (j * heads // (HQ // HK)) * DH
        v = HK * DH + k
        kv_send[j, :tokens, :] = kv_ref[:, k : k + DH]
        kv_send[j, tokens : 2 * tokens, :] = kv_ref[:, v : v + DH]
        kv_send[j, 2 * tokens :, :] = numbers
    departures[0].start()
    for kind, ref in ((0, q_ref), (1, g_ref)):
        arrivals[2 + kind].wait()
        for h in range(HQ):
            to = jnp.bitwise_xor(line, h // heads)
            q_send[to, kind * heads + h % heads] = ref[:, h * DH : (h + 1) * DH]
    for copy in departures[1 : 1 + lines]:
        copy.start()
    arrivals[4].wait()
    span = share * dp
    for s in range(width // share):
        turned = h_ref[:, s * span : (s + 1) * span].T
        for r in range(dp):
            part = turned[r * share : (r + 1) * share]
            cols_ref[jnp.bitwise_xor(core, r), s * share : (s + 1) * share, :] = part
    for copy in departures[1 + lines :]:
        copy.start()
    for copy in departures:
        copy.wait()


def gather_kernel(part_hbm, out_hbm, part_ref, out_ref, sems):
    planes, lines = part_ref.shape[0], part_ref.shape[1]
    arrivals = [
        pltpu.make_async_copy(part_hbm.at[w], part_ref.at[w], sems.at[w]) for w in range(planes)
    ]
    for copy in arrivals:
        copy.start()
    for copy in arrivals:
        copy.wait()
    for j in range(lines):
        total = part_ref[0, j].astype(jnp.float32)
        for w in range(1, planes):
            total += part_ref[w, j].astype(jnp.float32)
        out_ref[j] = total.astype(jnp.bfloat16)
    copy = pltpu.make_async_copy(out_ref, out_hbm, sems.at[planes])
    copy.start()
    copy.wait()


def combine_kernel(part_ref, out_ref):
    tokens = out_ref.shape[0]
    each = part_ref.shape[0] // HK
    for g in range(HK):
        for kind in range(2):
            rows = slice(kind * tokens, (kind + 1) * tokens)
            total = part_ref[g * each, rows, :].astype(jnp.float32)
            for j in range(g * each + 1, (g + 1) * each):
                total += part_ref[j, rows, :].astype(jnp.float32)
            at = (kind * HK + g) * DH
            out_ref[:, at : at + DH] = total.astype(jnp.bfloat16)


def weight_kernel(*refs):
    *cols_ref, kv_ref, out_hbm, out_ref, sems = refs
    mine = lax.axis_index("dp")
    seq, share = out_ref.shape[0], out_ref.shape[1]
    pieces = sems.shape[0]
    some = seq // pieces
    departures = []
    for j in range(pieces):
        to = pl.ds(j * some, some)
        departures.append(
            pltpu.make_async_copy(out_ref.at[to], out_hbm.at[to], sems.at[j])
        )
        at = slice(j * some * share, (j + 1) * some * share)
        total = dot(cols_ref[0][at], kv_ref[mine], NN)
        for r in range(1, len(cols_ref)):
            total += dot(cols_ref[r][at], kv_ref[jnp.bitwise_xor(mine, r)], NN)
        out_ref[j * some : (j + 1) * some] = total.astype(jnp.bfloat16).reshape(
            some, share, total.shape[1]
        )
        departures[j].start()
    for copy in departures:
        copy.wait()


def unpack_kernel(*refs):
    part_hbm, out_hbm, part_ref, out_ref, sems = refs[:-4], *refs[-4:]
    line = lax.axis_index("seq") // PLANES
    heads = part_ref.shape[1]
    arrivals = [
        pltpu.make_async_copy(part, part_ref.at[k], sems.at[k]) for k, part in enumerate(part_hbm)
    ]
    for copy in arrivals:
        copy.start()
    for k, copy in enumerate(arrivals):
        copy.wait()
        first = jnp.bitwise_xor(line, k) * heads
        for h in range(heads):
            at = pl.ds(pl.multiple_of((first + h) * DH, DH), DH)
            out_ref[:, at] = part_ref[k, h]
    copy = pltpu.make_async_copy(out_ref, out_hbm, sems.at[len(part_hbm)])
    copy.start()
    copy.wait()


def total_kernel(part_hbm, out_hbm, part_ref, out_ref, sems):
    seq = part_ref.shape[0]
    pieces = sems.shape[0] - 1
    some = seq // pieces
    arrivals = []
    for j in range(pieces):
        at = pl.ds(j * some, some)
        arrivals.append(pltpu.make_async_copy(part_hbm.at[at], part_ref.at[at], sems.at[j]))
    for copy in arrivals:
        copy.start()
    total = jnp.zeros(out_ref.shape, jnp.float32)
    for j in range(pieces):
        arrivals[j].wait()
        for s in range(j * some, (j + 1) * some):
            total += part_ref[s].astype(jnp.float32)
    out_ref[...] = total
    copy = pltpu.make_async_copy(out_ref, out_hbm, sems.at[pieces])
    copy.start()
    copy.wait()


def exchange(array, axis, groups=None):
    return lax.all_to_all(
        array, axis, split_axis=0, concat_axis=0, axis_index_groups=groups, tiled=True
    )


def shards(hidden, queries, keyvals, out_grad, segment):
    seq, dp = lax.axis_size("seq"), lax.axis_size("dp")
    tokens, width = hidden.shape[1], hidden.shape[2]
    share = width // (seq * dp)
    lines = seq // PLANES
    heads = HQ // lines
    half = jnp.bfloat16
    shape = jax.ShapeDtypeStruct
    along = [[j * PLANES + w for j in range(lines)] for w in range(PLANES)]
    across = [[j * PLANES + w for w in range(PLANES)] for j in range(lines)]

    def partners(k):
        return [(p, (p // PLANES ^ k) * PLANES + p % PLANES) for p in range(seq)]

    inputs = [queries[0], out_grad[0], keyvals[0], segment, hidden[0]]
    shared = (lines, 2 * tokens + SEGMENT_ROWS, DH)
    kv, *parts = local(
        pack_kernel,
        (shape(shared, half),)
        + (shape((2 * heads, tokens, DH), half),) * lines
        + (shape((seq * share, tokens), half),) * dp,
        inputs,
        [
            pltpu.VMEM(queries.shape[1:], half),
            pltpu.VMEM(out_grad.shape[1:], half),
            pltpu.VMEM(keyvals.shape[1:], half),
            pltpu.VMEM(segment.shape, segment.dtype),
            pltpu.VMEM(hidden.shape[1:], half),
            pltpu.VMEM(shared, half),
            pltpu.VMEM((lines, 2 * heads, tokens, DH), half),
            pltpu.VMEM((dp, seq * share, tokens), half),
            pltpu.SemaphoreType.DMA((5,)),
            pltpu.SemaphoreType.DMA((1 + lines + dp,)),
        ],
        "pack",
    )
    parts, columns = parts[:lines], parts[lines:]
    kv, parts = lax.optimization_barrier((exchange(kv, "seq", along), parts))
    for k in range(1, lines):
        parts[k] = lax.ppermute(parts[k], "seq", partners(k))
    kv = jnp.broadcast_to(kv[None], (PLANES,) + shared)
    kv = exchange(kv, "seq", across)
    kv, parts, columns = lax.optimization_barrier((kv, parts, columns))
    for k in range(1, dp):
        columns[k] = lax.ppermute(columns[k], "dp", [(r, r ^ k) for r in range(dp)])
    dkv, *dq = attention(kv, parts)
    dkv, dq, columns = lax.optimization_barrier((dkv, dq, columns))
    for k in range(1, lines):
        dq[k] = lax.ppermute(dq[k], "seq", partners(k))
    dkv, dq = lax.optimization_barrier((exchange(dkv, "seq", across), dq))
    dkv = local(
        gather_kernel,
        shape((lines, 2 * tokens, DH), half),
        [dkv],
        [
            pltpu.VMEM(dkv.shape, half),
            pltpu.VMEM(dkv.shape[1:], half),
            pltpu.SemaphoreType.DMA((PLANES + 1,)),
        ],
        "gather",
    )
    dkv = exchange(dkv, "seq", along)
    keyval_grad = pl.pallas_call(
        combine_kernel,
        out_shape=shape((tokens, 2 * HK * DH), half),
        in_specs=[pl.BlockSpec(memory_space=pltpu.VMEM)],
        out_specs=pl.BlockSpec(memory_space=pltpu.VMEM),
        compiler_params=pltpu.CompilerParams(vmem_limit_bytes=SMALL_LIMIT),
        name="combine",
    )(dkv)
    every = lax.all_gather(keyval_grad, "dp", axis=0)
    result = (seq, share, 2 * HK * DH)
    partial = pl.pallas_call(
        weight_kernel,
        out_shape=shape(result, half),
        in_specs=[pl.BlockSpec(memory_space=pltpu.VMEM)] * (dp + 1),
        out_specs=pl.BlockSpec(memory_space=pltpu.HBM),
        scratch_shapes=[pltpu.VMEM(result, half), pltpu.SemaphoreType.DMA((4,))],
        compiler_params=pltpu.CompilerParams(vmem_limit_bytes=SMALL_LIMIT),
        name="weight",
    )(*columns, every)
    partial = exchange(partial, "seq")
    query_grad = local(
        unpack_kernel,
        shape((tokens, HQ * DH), half),
        dq,
        [
            pltpu.VMEM((lines, heads, tokens, DH), half),
            pltpu.VMEM((tokens, HQ * DH), half),
            pltpu.SemaphoreType.DMA((lines + 1,)),
        ],
        "unpack",
    )
    weight_grad = local(
        total_kernel,
        shape(result[1:], jnp.float32),
        [partial],
        [
            pltpu.VMEM(result, half),
            pltpu.VMEM(result[1:], jnp.float32),
            pltpu.SemaphoreType.DMA((5,)),
        ],
        "total",
    )
    return (query_grad[None], keyval_grad[None], weight_grad)


def solution(mesh):
    in_specs = (
        P("dp", "seq", None),
        P("dp", "seq", None),
        P("dp", "seq", None),
        P("dp", "seq", None),
        P("dp", "seq"),
    )
    out_specs = (P("dp", "seq", None), P("dp", "seq", None), P(("seq", "dp"), None))
    return jax.shard_map(shards, mesh=mesh, in_specs=in_specs, out_specs=out_specs, check_vma=False)
```

```python
import jax
import jax.numpy as jnp
from jax import lax
from jax.experimental import pallas as pl
from jax.experimental.pallas import tpu as pltpu
from jax.sharding import PartitionSpec as P

HQ = 32
HK = 2
DH = 128
SCALE = DH ** -0.5
EXP2_SCALE = SCALE * 1.4426950408889634
MASKED = -1e30
LOWEST = -1e29
SEGMENT_ROWS = 16
BQ = 1024
UNIT = 256
CHUNKS = (4, 2, 1)
PLANES = 8
VMEM_LIMIT = 127 * 512 * 1024
SMALL_LIMIT = 20 * 1024 * 1024
ATTENTION_LIMIT = 59 * 1024 * 1024
NT = (((1,), (1,)), ((), ()))
NN = (((1,), (0,)), ((), ()))


def dot(a, b, dims):
    return lax.dot_general(a, b, dims, preferred_element_type=jnp.float32)


def attention_kernel(*refs):
    kv_hbm, q_hbm = refs[0], refs[1:5]
    dkv_hbm, dq_hbm = refs[5], refs[6:10]
    x_ref, seg_ref, q_ref, dq_ref, dkv_ref = refs[10:15]
    p_ref, dp_ref, m_ref, dk_ref, dv_ref, kt_ref, sems, out_sems = refs[15:]
    planes, lines = kv_hbm.shape[0], kv_hbm.shape[1]
    blocks = planes * lines
    seq = blocks * 128
    un = UNIT // 128
    mine = lax.axis_index("seq")
    line, plane = mine // planes, mine % planes

    arrivals = []
    for j in range(lines):
        at = pl.ds(j * planes, planes)
        arrivals.append(
            pltpu.make_async_copy(kv_hbm.at[:, j, 256:], seg_ref.at[at], sems.at[j])
        )
    for j in range(lines):
        at = pl.ds(j * planes, planes)
        arrivals.append(
            pltpu.make_async_copy(kv_hbm.at[:, j, :256], x_ref.at[at], sems.at[lines + j])
        )
    for j in range(lines):
        arrivals.append(pltpu.make_async_copy(q_hbm[j], q_ref.at[j], sems.at[2 * lines + j]))
    for copy in arrivals:
        copy.start()

    def departure(j):
        return pltpu.make_async_copy(dq_ref.at[j], dq_hbm[j], out_sems.at[j])

    def final(j):
        return pltpu.make_async_copy(dkv_ref.at[:, j], dkv_hbm.at[:, j], out_sems.at[lines + j])

    dk_ref[...] = jnp.zeros_like(dk_ref)
    dv_ref[...] = jnp.zeros_like(dv_ref)
    for copy in arrivals:
        copy.wait()

    def rows(first, count, slot):
        part = x_ref[pl.ds(first, count), slot * 128 : (slot + 1) * 128, :]
        return part.reshape(count * 128, DH)

    def turn(b, _):
        kt_ref[:, pl.ds(pl.multiple_of(b * 128, 128), 128)] = x_ref[b, :128, :].T
        return 0

    lax.fori_loop(0, blocks, turn, 0)
    segments = seg_ref[:, 0:1, :].astype(jnp.float32)
    count0 = jnp.sum(jnp.where(segments < 0.5, 1.0, 0.0)).astype(jnp.int32)
    count1 = jnp.sum(jnp.where(segments < 1.5, 1.0, 0.0)).astype(jnp.int32)

    def start_of(pos):
        return jnp.where(pos >= count1, count1, jnp.where(pos >= count0, count0, 0))

    heads = dq_ref.shape[1]
    some = BQ // 128
    turns = heads // some

    def query_block(i, _):
        j, part = i // turns, i % turns
        first = (jnp.bitwise_xor(line, j) * planes + plane) * 128
        q = q_ref[j, pl.ds(part * some, some)].reshape(BQ, DH)
        cotan = q_ref[j, pl.ds(heads + part * some, some)].reshape(BQ, DH)
        qpos = first + lax.broadcasted_iota(jnp.int32, (1, BQ), 1) % 128
        qstart = start_of(qpos)
        low = start_of(first) // UNIT
        high = (first + 127) // UNIT + 1

        def walk(body, state):
            at = low
            for size in CHUNKS:
                count = (high - at) // size

                def step(t, carry, size=size, at=at):
                    return body(at + t * size, size, carry)

                state = lax.fori_loop(0, count, step, state)
                at = at + count * size
            return state

        def scores(kb, size, carry):
            plain = ((kb + size) * UNIT <= first) & (kb * UNIT >= start_of(first + 127))
            return lax.cond(
                plain,
                lambda c: score_part(kb, size, c, False),
                lambda c: score_part(kb, size, c, True),
                carry,
            )

        def score_part(kb, size, carry, masked):
            top, total, delta = carry
            k = rows(kb * un, size * un, 0)
            v = rows(kb * un, size * un, 1)
            st = dot(k, q, NT)
            dpt = dot(v, cotan, NT)
            at = pl.ds(pl.multiple_of(kb * UNIT, UNIT), size * UNIT)
            if masked:
                kpos = kb * UNIT + lax.broadcasted_iota(jnp.int32, (size * UNIT, BQ), 0)
                st = jnp.where((kpos >= qstart) & (kpos <= qpos), st, MASKED)
            newtop = jnp.maximum(top, jnp.max(st, axis=0, keepdims=True))
            p = jnp.exp2((st - newtop) * EXP2_SCALE)
            fade = jnp.exp2((top - newtop) * EXP2_SCALE)
            total = total * fade + jnp.sum(p, axis=0, keepdims=True)
            delta = delta * fade + jnp.sum(p * dpt, axis=0, keepdims=True)
            p_ref[at, :] = p
            dp_ref[at, :] = dpt
            m_ref[pl.ds(kb, 1), :] = newtop
            return newtop, total, delta

        zero = jnp.zeros((1, BQ), jnp.float32)
        top, total, delta = walk(scores, (zero + LOWEST, zero, zero))
        inverse = 1.0 / total
        delta = delta * inverse

        def grads(kb, size, dq):
            at = pl.ds(pl.multiple_of(kb * UNIT, UNIT), size * UNIT)
            factor = jnp.exp2((m_ref[pl.ds(kb, 1), :] - top) * EXP2_SCALE) * inverse
            w = p_ref[at, :] * factor
            ds = (w * (dp_ref[at, :] - delta)).astype(jnp.bfloat16)
            dv_ref[at, :] += dot(w.astype(jnp.bfloat16), cotan, NN)
            dk_ref[at, :] += dot(ds, q, NN)
            return dq + dot(kt_ref[:, at], ds, NN)

        dq = walk(grads, jnp.zeros((DH, BQ), jnp.float32)).T
        dq_ref[j, pl.ds(part * some, some)] = (
            (dq * SCALE).astype(jnp.bfloat16).reshape(some, 128, DH)
        )
        for k in range(lines):
            pl.when(i == (k + 1) * turns - 1)(departure(k).start)
        return 0

    lax.fori_loop(0, lines * turns, query_block, 0)

    def finish(b, _):
        at = pl.ds(pl.multiple_of(b * 128, 128), 128)
        dkv_ref[b % planes, b // planes, :128, :] = (dk_ref[at, :] * SCALE).astype(jnp.bfloat16)
        dkv_ref[b % planes, b // planes, 128:, :] = dv_ref[at, :].astype(jnp.bfloat16)
        return 0

    for j in range(lines):
        lax.fori_loop(j * planes, (j + 1) * planes, finish, 0)
        final(j).start()
    for j in range(lines):
        departure(j).wait()
        final(j).wait()


def local(body, out_shape, inputs, scratch, name):
    spec = pl.BlockSpec(memory_space=pltpu.HBM)
    many = isinstance(out_shape, tuple)
    return pl.pallas_call(
        body,
        out_shape=out_shape,
        in_specs=[spec] * len(inputs),
        out_specs=(spec,) * len(out_shape) if many else spec,
        scratch_shapes=scratch,
        compiler_params=pltpu.CompilerParams(vmem_limit_bytes=VMEM_LIMIT),
        name=name,
    )(*inputs)


def attention(kv, parts):
    planes, lines = kv.shape[0], kv.shape[1]
    blocks = planes * lines
    seq = blocks * 128
    heads = parts[0].shape[0] // 2
    half = jnp.bfloat16
    shape = jax.ShapeDtypeStruct
    spec = pl.BlockSpec(memory_space=pltpu.HBM)
    return pl.pallas_call(
        attention_kernel,
        out_shape=(shape((planes, lines, 256, DH), half),)
        + (shape((heads, 128, DH), half),) * lines,
        in_specs=[spec] * (1 + lines),
        out_specs=(spec,) * (1 + lines),
        scratch_shapes=[
            pltpu.VMEM((blocks, 256, DH), half),
            pltpu.VMEM((blocks, SEGMENT_ROWS, 128), half),
            pltpu.VMEM((lines, 2 * heads, 128, DH), half),
            pltpu.VMEM((lines, heads, 128, DH), half),
            pltpu.VMEM((planes, lines, 256, DH), half),
            pltpu.VMEM((seq, BQ), jnp.float32),
            pltpu.VMEM((seq, BQ), jnp.float32),
            pltpu.VMEM((max(8, seq // UNIT), BQ), jnp.float32),
            pltpu.VMEM((seq, DH), jnp.float32),
            pltpu.VMEM((seq, DH), jnp.float32),
            pltpu.VMEM((DH, seq), half),
            pltpu.SemaphoreType.DMA((3 * lines,)),
            pltpu.SemaphoreType.DMA((2 * lines,)),
        ],
        compiler_params=pltpu.CompilerParams(vmem_limit_bytes=ATTENTION_LIMIT),
        cost_estimate=pl.CostEstimate(
            flops=10 * 1000**3, bytes_accessed=8 * 1000**2, transcendentals=8 * 1000**2
        ),
        name="attention",
    )(kv, *parts)


def pack_kernel(q_hbm, g_hbm, kv_hbm, seg_hbm, h_hbm, *rest):
    kv_out, q_out, cols_out = rest[0], rest[1:5], rest[5:9]
    q_ref, g_ref, kv_ref, seg_ref, h_ref, kv_send, q_send, cols_ref, in_sems, out_sems = rest[9:]
    line, core = lax.axis_index("seq") // PLANES, lax.axis_index("dp")
    pairs = [(seg_hbm, seg_ref), (kv_hbm, kv_ref), (q_hbm, q_ref), (g_hbm, g_ref), (h_hbm, h_ref)]
    arrivals = [pltpu.make_async_copy(*pair, in_sems.at[i]) for i, pair in enumerate(pairs)]
    for copy in arrivals:
        copy.start()
    tokens = q_ref.shape[0]
    lines, heads = q_send.shape[0], q_send.shape[1] // 2
    dp, width = cols_ref.shape[0], cols_ref.shape[1]
    share = h_ref.shape[1] // (HQ * dp)
    departures = [pltpu.make_async_copy(kv_send, kv_out, out_sems.at[0])]
    for k in range(lines):
        departures.append(pltpu.make_async_copy(q_send.at[k], q_out[k], out_sems.at[1 + k]))
    for k in range(dp):
        sem = out_sems.at[1 + lines + k]
        departures.append(pltpu.make_async_copy(cols_ref.at[k], cols_out[k], sem))
    arrivals[0].wait()
    numbers = jnp.broadcast_to(seg_ref[...].astype(jnp.bfloat16), (SEGMENT_ROWS, tokens))
    arrivals[1].wait()
    for j in range(lines):
        k = (j * heads // (HQ // HK)) * DH
        v = HK * DH + k
        kv_send[j, :tokens, :] = kv_ref[:, k : k + DH]
        kv_send[j, tokens : 2 * tokens, :] = kv_ref[:, v : v + DH]
        kv_send[j, 2 * tokens :, :] = numbers
    departures[0].start()
    for kind, ref in ((0, q_ref), (1, g_ref)):
        arrivals[2 + kind].wait()
        for h in range(HQ):
            to = jnp.bitwise_xor(line, h // heads)
            q_send[to, kind * heads + h % heads] = ref[:, h * DH : (h + 1) * DH]
    for copy in departures[1 : 1 + lines]:
        copy.start()
    arrivals[4].wait()
    span = share * dp
    for s in range(width // share):
        turned = h_ref[:, s * span : (s + 1) * span].T
        for r in range(dp):
            part = turned[r * share : (r + 1) * share]
            cols_ref[jnp.bitwise_xor(core, r), s * share : (s + 1) * share, :] = part
    for copy in departures[1 + lines :]:
        copy.start()
    for copy in departures:
        copy.wait()


def gather_kernel(part_hbm, out_hbm, part_ref, out_ref, sems):
    planes, lines = part_ref.shape[0], part_ref.shape[1]
    arrivals = [
        pltpu.make_async_copy(part_hbm.at[w], part_ref.at[w], sems.at[w]) for w in range(planes)
    ]
    for copy in arrivals:
        copy.start()
    for copy in arrivals:
        copy.wait()
    for j in range(lines):
        total = part_ref[0, j].astype(jnp.float32)
        for w in range(1, planes):
            total += part_ref[w, j].astype(jnp.float32)
        out_ref[j] = total.astype(jnp.bfloat16)
    copy = pltpu.make_async_copy(out_ref, out_hbm, sems.at[planes])
    copy.start()
    copy.wait()


def combine_kernel(part_ref, out_ref):
    tokens = out_ref.shape[0]
    each = part_ref.shape[0] // HK
    for g in range(HK):
        for kind in range(2):
            rows = slice(kind * tokens, (kind + 1) * tokens)
            total = part_ref[g * each, rows, :].astype(jnp.float32)
            for j in range(g * each + 1, (g + 1) * each):
                total += part_ref[j, rows, :].astype(jnp.float32)
            at = (kind * HK + g) * DH
            out_ref[:, at : at + DH] = total.astype(jnp.bfloat16)


def weight_kernel(*refs):
    cols_hbm, (kv_hbm, out_hbm, cols_ref, kv_ref, out_ref, sems) = refs[:-6], refs[-6:]
    mine = lax.axis_index("dp")
    dp = len(cols_hbm)
    seq, share = out_ref.shape[0], out_ref.shape[1]
    pieces = 4
    some = seq // pieces
    rows = some * share
    first = pltpu.make_async_copy(kv_hbm, kv_ref, sems.at[0])
    first.start()
    arrivals, departures = [], []
    for j in range(pieces):
        at, to = pl.ds(j * rows, rows), pl.ds(j * some, some)
        for r in range(dp):
            sem = sems.at[1 + j * dp + r]
            arrivals.append(
                pltpu.make_async_copy(cols_hbm[r].at[at], cols_ref.at[r, at], sem)
            )
        sem = sems.at[1 + pieces * dp + j]
        departures.append(pltpu.make_async_copy(out_ref.at[to], out_hbm.at[to], sem))
    for copy in arrivals:
        copy.start()
    first.wait()
    for j in range(pieces):
        total = None
        for r in range(dp):
            arrivals[j * dp + r].wait()
            part = dot(
                cols_ref[r, j * rows : (j + 1) * rows], kv_ref[jnp.bitwise_xor(mine, r)], NN
            )
            total = part if total is None else total + part
        out_ref[j * some : (j + 1) * some] = total.astype(jnp.bfloat16).reshape(
            some, share, total.shape[1]
        )
        departures[j].start()
    for copy in departures:
        copy.wait()


def unpack_kernel(*refs):
    part_hbm, out_hbm, part_ref, out_ref, sems = refs[:-4], *refs[-4:]
    line = lax.axis_index("seq") // PLANES
    heads = part_ref.shape[1]
    arrivals = [
        pltpu.make_async_copy(part, part_ref.at[k], sems.at[k]) for k, part in enumerate(part_hbm)
    ]
    for copy in arrivals:
        copy.start()
    for k, copy in enumerate(arrivals):
        copy.wait()
        first = jnp.bitwise_xor(line, k) * heads
        for h in range(heads):
            at = pl.ds(pl.multiple_of((first + h) * DH, DH), DH)
            out_ref[:, at] = part_ref[k, h]
    copy = pltpu.make_async_copy(out_ref, out_hbm, sems.at[len(part_hbm)])
    copy.start()
    copy.wait()


def total_kernel(part_hbm, out_hbm, part_ref, out_ref, sems):
    seq = part_ref.shape[0]
    pieces = sems.shape[0] - 1
    some = seq // pieces
    arrivals = []
    for j in range(pieces):
        at = pl.ds(j * some, some)
        arrivals.append(pltpu.make_async_copy(part_hbm.at[at], part_ref.at[at], sems.at[j]))
    for copy in arrivals:
        copy.start()
    total = jnp.zeros(out_ref.shape, jnp.float32)
    for j in range(pieces):
        arrivals[j].wait()
        for s in range(j * some, (j + 1) * some):
            total += part_ref[s].astype(jnp.float32)
    out_ref[...] = total
    copy = pltpu.make_async_copy(out_ref, out_hbm, sems.at[pieces])
    copy.start()
    copy.wait()


def exchange(array, axis, groups=None):
    return lax.all_to_all(
        array, axis, split_axis=0, concat_axis=0, axis_index_groups=groups, tiled=True
    )


def shards(hidden, queries, keyvals, out_grad, segment):
    seq, dp = lax.axis_size("seq"), lax.axis_size("dp")
    tokens, width = hidden.shape[1], hidden.shape[2]
    share = width // (seq * dp)
    lines = seq // PLANES
    heads = HQ // lines
    half = jnp.bfloat16
    shape = jax.ShapeDtypeStruct
    along = [[j * PLANES + w for j in range(lines)] for w in range(PLANES)]
    across = [[j * PLANES + w for w in range(PLANES)] for j in range(lines)]

    def partners(k):
        return [(p, (p // PLANES ^ k) * PLANES + p % PLANES) for p in range(seq)]

    inputs = [queries[0], out_grad[0], keyvals[0], segment, hidden[0]]
    shared = (lines, 2 * tokens + SEGMENT_ROWS, DH)
    kv, *parts = local(
        pack_kernel,
        (shape(shared, half),)
        + (shape((2 * heads, tokens, DH), half),) * lines
        + (shape((seq * share, tokens), half),) * dp,
        inputs,
        [
            pltpu.VMEM(queries.shape[1:], half),
            pltpu.VMEM(out_grad.shape[1:], half),
            pltpu.VMEM(keyvals.shape[1:], half),
            pltpu.VMEM(segment.shape, segment.dtype),
            pltpu.VMEM(hidden.shape[1:], half),
            pltpu.VMEM(shared, half),
            pltpu.VMEM((lines, 2 * heads, tokens, DH), half),
            pltpu.VMEM((dp, seq * share, tokens), half),
            pltpu.SemaphoreType.DMA((5,)),
            pltpu.SemaphoreType.DMA((1 + lines + dp,)),
        ],
        "pack",
    )
    parts, columns = parts[:lines], parts[lines:]
    kv, parts = lax.optimization_barrier((exchange(kv, "seq", along), parts))
    for k in range(1, lines):
        parts[k] = lax.ppermute(parts[k], "seq", partners(k))
    kv = jnp.broadcast_to(kv[None], (PLANES,) + shared)
    kv = exchange(kv, "seq", across)
    kv, parts, columns = lax.optimization_barrier((kv, parts, columns))
    for k in range(1, dp):
        columns[k] = lax.ppermute(columns[k], "dp", [(r, r ^ k) for r in range(dp)])
    dkv, *dq = attention(kv, parts)
    dkv, dq, columns = lax.optimization_barrier((dkv, dq, columns))
    for k in range(1, lines):
        dq[k] = lax.ppermute(dq[k], "seq", partners(k))
    dkv, dq = lax.optimization_barrier((exchange(dkv, "seq", across), dq))
    dkv = local(
        gather_kernel,
        shape((lines, 2 * tokens, DH), half),
        [dkv],
        [
            pltpu.VMEM(dkv.shape, half),
            pltpu.VMEM(dkv.shape[1:], half),
            pltpu.SemaphoreType.DMA((PLANES + 1,)),
        ],
        "gather",
    )
    dkv = exchange(dkv, "seq", along)
    keyval_grad = pl.pallas_call(
        combine_kernel,
        out_shape=shape((tokens, 2 * HK * DH), half),
        in_specs=[pl.BlockSpec(memory_space=pltpu.VMEM)],
        out_specs=pl.BlockSpec(memory_space=pltpu.VMEM),
        compiler_params=pltpu.CompilerParams(vmem_limit_bytes=SMALL_LIMIT),
        name="combine",
    )(dkv)
    every = lax.all_gather(keyval_grad, "dp", axis=0)
    result = (seq, share, 2 * HK * DH)
    partial = local(
        weight_kernel,
        shape(result, half),
        [*columns, every],
        [
            pltpu.VMEM((dp, seq * share, tokens), half),
            pltpu.VMEM(every.shape, half),
            pltpu.VMEM(result, half),
            pltpu.SemaphoreType.DMA((1 + 4 * dp + 4,)),
        ],
        "weight",
    )
    partial = exchange(partial, "seq")
    query_grad = local(
        unpack_kernel,
        shape((tokens, HQ * DH), half),
        dq,
        [
            pltpu.VMEM((lines, heads, tokens, DH), half),
            pltpu.VMEM((tokens, HQ * DH), half),
            pltpu.SemaphoreType.DMA((lines + 1,)),
        ],
        "unpack",
    )
    weight_grad = local(
        total_kernel,
        shape(result[1:], jnp.float32),
        [partial],
        [
            pltpu.VMEM(result, half),
            pltpu.VMEM(result[1:], jnp.float32),
            pltpu.SemaphoreType.DMA((5,)),
        ],
        "total",
    )
    return (query_grad[None], keyval_grad[None], weight_grad)


def solution(mesh):
    in_specs = (
        P("dp", "seq", None),
        P("dp", "seq", None),
        P("dp", "seq", None),
        P("dp", "seq", None),
        P("dp", "seq"),
    )
    out_specs = (P("dp", "seq", None), P("dp", "seq", None), P(("seq", "dp"), None))
    return jax.shard_map(shards, mesh=mesh, in_specs=in_specs, out_specs=out_specs, check_vma=False)
```

```python
import jax
import jax.numpy as jnp
from jax import lax
from jax.experimental import pallas as pl
from jax.experimental.pallas import tpu as pltpu
from jax.sharding import PartitionSpec as P

HQ = 32
HK = 2
DH = 128
SCALE = DH ** -0.5
EXP2_SCALE = SCALE * 1.4426950408889634
MASKED = -1e30
LOWEST = -1e29
SEGMENT_ROWS = 16
BQ = 1024
UNIT = 256
CHUNKS = (4, 2, 1)
PLANES = 8
VMEM_LIMIT = 127 * 512 * 1024
SMALL_LIMIT = 20 * 1024 * 1024
ATTENTION_LIMIT = 59 * 1024 * 1024
NT = (((1,), (1,)), ((), ()))
NN = (((1,), (0,)), ((), ()))


def dot(a, b, dims):
    return lax.dot_general(a, b, dims, preferred_element_type=jnp.float32)


def attention_kernel(*refs):
    kv_hbm, q_hbm = refs[0], refs[1:5]
    dkv_hbm, dq_hbm = refs[5], refs[6:10]
    x_ref, seg_ref, q_ref, dq_ref, dkv_ref = refs[10:15]
    p_ref, dp_ref, m_ref, dk_ref, dv_ref, kt_ref, sems, out_sems = refs[15:]
    planes, lines = kv_hbm.shape[0], kv_hbm.shape[1]
    blocks = planes * lines
    seq = blocks * 128
    un = UNIT // 128
    mine = lax.axis_index("seq")
    line, plane = mine // planes, mine % planes

    arrivals = []
    for j in range(lines):
        at = pl.ds(j * planes, planes)
        arrivals.append(
            pltpu.make_async_copy(kv_hbm.at[:, j, 256:], seg_ref.at[at], sems.at[j])
        )
    for j in range(lines):
        at = pl.ds(j * planes, planes)
        arrivals.append(
            pltpu.make_async_copy(kv_hbm.at[:, j, :256], x_ref.at[at], sems.at[lines + j])
        )
    for j in range(lines):
        arrivals.append(pltpu.make_async_copy(q_hbm[j], q_ref.at[j], sems.at[2 * lines + j]))
    for copy in arrivals:
        copy.start()

    def departure(j):
        return pltpu.make_async_copy(dq_ref.at[j], dq_hbm[j], out_sems.at[j])

    def final(j):
        return pltpu.make_async_copy(dkv_ref.at[:, j], dkv_hbm.at[:, j], out_sems.at[lines + j])

    dk_ref[...] = jnp.zeros_like(dk_ref)
    dv_ref[...] = jnp.zeros_like(dv_ref)
    for copy in arrivals[: 2 * lines]:
        copy.wait()

    def rows(first, count, slot):
        part = x_ref[pl.ds(first, count), slot * 128 : (slot + 1) * 128, :]
        return part.reshape(count * 128, DH)

    def turn(b, _):
        kt_ref[:, pl.ds(pl.multiple_of(b * 128, 128), 128)] = x_ref[b, :128, :].T
        return 0

    lax.fori_loop(0, blocks, turn, 0)
    segments = seg_ref[:, 0:1, :].astype(jnp.float32)
    count0 = jnp.sum(jnp.where(segments < 0.5, 1.0, 0.0)).astype(jnp.int32)
    count1 = jnp.sum(jnp.where(segments < 1.5, 1.0, 0.0)).astype(jnp.int32)

    def start_of(pos):
        return jnp.where(pos >= count1, count1, jnp.where(pos >= count0, count0, 0))

    heads = dq_ref.shape[1]
    some = BQ // 128
    turns = heads // some

    def query_block(i, _):
        j, part = i // turns, i % turns
        for k in range(lines):
            pl.when(i == k * turns)(arrivals[2 * lines + k].wait)
        first = (jnp.bitwise_xor(line, j) * planes + plane) * 128
        q = q_ref[j, pl.ds(part * some, some)].reshape(BQ, DH)
        cotan = q_ref[j, pl.ds(heads + part * some, some)].reshape(BQ, DH)
        qpos = first + lax.broadcasted_iota(jnp.int32, (1, BQ), 1) % 128
        qstart = start_of(qpos)
        low = start_of(first) // UNIT
        high = (first + 127) // UNIT + 1

        def walk(body, state):
            at = low
            for size in CHUNKS:
                count = (high - at) // size

                def step(t, carry, size=size, at=at):
                    return body(at + t * size, size, carry)

                state = lax.fori_loop(0, count, step, state)
                at = at + count * size
            return state

        def scores(kb, size, carry):
            plain = ((kb + size) * UNIT <= first) & (kb * UNIT >= start_of(first + 127))
            return lax.cond(
                plain,
                lambda c: score_part(kb, size, c, False),
                lambda c: score_part(kb, size, c, True),
                carry,
            )

        def score_part(kb, size, carry, masked):
            top, total, delta = carry
            k = rows(kb * un, size * un, 0)
            v = rows(kb * un, size * un, 1)
            st = dot(k, q, NT)
            dpt = dot(v, cotan, NT)
            at = pl.ds(pl.multiple_of(kb * UNIT, UNIT), size * UNIT)
            if masked:
                kpos = kb * UNIT + lax.broadcasted_iota(jnp.int32, (size * UNIT, BQ), 0)
                st = jnp.where((kpos >= qstart) & (kpos <= qpos), st, MASKED)
            newtop = jnp.maximum(top, jnp.max(st, axis=0, keepdims=True))
            p = jnp.exp2((st - newtop) * EXP2_SCALE)
            fade = jnp.exp2((top - newtop) * EXP2_SCALE)
            total = total * fade + jnp.sum(p, axis=0, keepdims=True)
            delta = delta * fade + jnp.sum(p * dpt, axis=0, keepdims=True)
            p_ref[at, :] = p
            dp_ref[at, :] = dpt
            m_ref[pl.ds(kb, 1), :] = newtop
            return newtop, total, delta

        zero = jnp.zeros((1, BQ), jnp.float32)
        top, total, delta = walk(scores, (zero + LOWEST, zero, zero))
        inverse = 1.0 / total
        delta = delta * inverse

        def grads(kb, size, dq):
            at = pl.ds(pl.multiple_of(kb * UNIT, UNIT), size * UNIT)
            factor = jnp.exp2((m_ref[pl.ds(kb, 1), :] - top) * EXP2_SCALE) * inverse
            w = p_ref[at, :] * factor
            ds = (w * (dp_ref[at, :] - delta)).astype(jnp.bfloat16)
            dv_ref[at, :] += dot(w.astype(jnp.bfloat16), cotan, NN)
            dk_ref[at, :] += dot(ds, q, NN)
            return dq + dot(kt_ref[:, at], ds, NN)

        dq = walk(grads, jnp.zeros((DH, BQ), jnp.float32)).T
        dq_ref[j, pl.ds(part * some, some)] = (
            (dq * SCALE).astype(jnp.bfloat16).reshape(some, 128, DH)
        )
        for k in range(lines):
            pl.when(i == (k + 1) * turns - 1)(departure(k).start)
        return 0

    lax.fori_loop(0, lines * turns, query_block, 0)

    def finish(b, _):
        at = pl.ds(pl.multiple_of(b * 128, 128), 128)
        dkv_ref[b % planes, b // planes, :128, :] = (dk_ref[at, :] * SCALE).astype(jnp.bfloat16)
        dkv_ref[b % planes, b // planes, 128:, :] = dv_ref[at, :].astype(jnp.bfloat16)
        return 0

    for j in range(lines):
        lax.fori_loop(j * planes, (j + 1) * planes, finish, 0)
        final(j).start()
    for j in range(lines):
        departure(j).wait()
        final(j).wait()


def local(body, out_shape, inputs, scratch, name):
    spec = pl.BlockSpec(memory_space=pltpu.HBM)
    many = isinstance(out_shape, tuple)
    return pl.pallas_call(
        body,
        out_shape=out_shape,
        in_specs=[spec] * len(inputs),
        out_specs=(spec,) * len(out_shape) if many else spec,
        scratch_shapes=scratch,
        compiler_params=pltpu.CompilerParams(vmem_limit_bytes=VMEM_LIMIT),
        name=name,
    )(*inputs)


def attention(kv, parts):
    planes, lines = kv.shape[0], kv.shape[1]
    blocks = planes * lines
    seq = blocks * 128
    heads = parts[0].shape[0] // 2
    half = jnp.bfloat16
    shape = jax.ShapeDtypeStruct
    spec = pl.BlockSpec(memory_space=pltpu.HBM)
    return pl.pallas_call(
        attention_kernel,
        out_shape=(shape((planes, lines, 256, DH), half),)
        + (shape((heads, 128, DH), half),) * lines,
        in_specs=[spec] * (1 + lines),
        out_specs=(spec,) * (1 + lines),
        scratch_shapes=[
            pltpu.VMEM((blocks, 256, DH), half),
            pltpu.VMEM((blocks, SEGMENT_ROWS, 128), half),
            pltpu.VMEM((lines, 2 * heads, 128, DH), half),
            pltpu.VMEM((lines, heads, 128, DH), half),
            pltpu.VMEM((planes, lines, 256, DH), half),
            pltpu.VMEM((seq, BQ), jnp.float32),
            pltpu.VMEM((seq, BQ), jnp.float32),
            pltpu.VMEM((max(8, seq // UNIT), BQ), jnp.float32),
            pltpu.VMEM((seq, DH), jnp.float32),
            pltpu.VMEM((seq, DH), jnp.float32),
            pltpu.VMEM((DH, seq), half),
            pltpu.SemaphoreType.DMA((3 * lines,)),
            pltpu.SemaphoreType.DMA((2 * lines,)),
        ],
        compiler_params=pltpu.CompilerParams(vmem_limit_bytes=ATTENTION_LIMIT),
        cost_estimate=pl.CostEstimate(
            flops=10 * 1000**3, bytes_accessed=8 * 1000**2, transcendentals=8 * 1000**2
        ),
        name="attention",
    )(kv, *parts)


def share_kernel(kv_hbm, seg_hbm, out_hbm, kv_ref, seg_ref, out_ref, sems):
    pairs = [(seg_hbm, seg_ref), (kv_hbm, kv_ref)]
    arrivals = [pltpu.make_async_copy(*pair, sems.at[i]) for i, pair in enumerate(pairs)]
    for copy in arrivals:
        copy.start()
    tokens = kv_ref.shape[0]
    lines = out_ref.shape[0]
    arrivals[0].wait()
    numbers = jnp.broadcast_to(seg_ref[...].astype(jnp.bfloat16), (SEGMENT_ROWS, tokens))
    arrivals[1].wait()
    for j in range(lines):
        k = (j * HK // lines) * DH
        v = HK * DH + k
        out_ref[j, :tokens, :] = kv_ref[:, k : k + DH]
        out_ref[j, tokens : 2 * tokens, :] = kv_ref[:, v : v + DH]
        out_ref[j, 2 * tokens :, :] = numbers
    copy = pltpu.make_async_copy(out_ref, out_hbm, sems.at[2])
    copy.start()
    copy.wait()


def pack_kernel(q_hbm, g_hbm, h_hbm, *rest):
    q_out, cols_out = rest[:4], rest[4:8]
    q_ref, g_ref, h_ref, q_send, cols_ref, in_sems, out_sems = rest[8:]
    line, core = lax.axis_index("seq") // PLANES, lax.axis_index("dp")
    pairs = [(q_hbm, q_ref), (g_hbm, g_ref), (h_hbm, h_ref)]
    arrivals = [pltpu.make_async_copy(*pair, in_sems.at[i]) for i, pair in enumerate(pairs)]
    for copy in arrivals:
        copy.start()
    lines, heads = q_send.shape[0], q_send.shape[1] // 2
    dp, width = cols_ref.shape[0], cols_ref.shape[1]
    share = h_ref.shape[1] // (HQ * dp)
    departures = []
    for k in range(lines):
        departures.append(pltpu.make_async_copy(q_send.at[k], q_out[k], out_sems.at[k]))
    for k in range(dp):
        sem = out_sems.at[lines + k]
        departures.append(pltpu.make_async_copy(cols_ref.at[k], cols_out[k], sem))
    for kind, ref in ((0, q_ref), (1, g_ref)):
        arrivals[kind].wait()
        for h in range(HQ):
            to = jnp.bitwise_xor(line, h // heads)
            q_send[to, kind * heads + h % heads] = ref[:, h * DH : (h + 1) * DH]
    for copy in departures[:lines]:
        copy.start()
    arrivals[2].wait()
    span = share * dp
    for s in range(width // share):
        turned = h_ref[:, s * span : (s + 1) * span].T
        for r in range(dp):
            part = turned[r * share : (r + 1) * share]
            cols_ref[jnp.bitwise_xor(core, r), s * share : (s + 1) * share, :] = part
    for copy in departures[lines:]:
        copy.start()
    for copy in departures:
        copy.wait()


def gather_kernel(part_hbm, out_hbm, part_ref, out_ref, sems):
    planes, lines = part_ref.shape[0], part_ref.shape[1]
    arrivals = [
        pltpu.make_async_copy(part_hbm.at[:, j], part_ref.at[:, j], sems.at[j])
        for j in range(lines)
    ]
    for copy in arrivals:
        copy.start()
    departures = []
    for j in range(lines):
        arrivals[j].wait()
        total = part_ref[0, j].astype(jnp.float32)
        for w in range(1, planes):
            total += part_ref[w, j].astype(jnp.float32)
        out_ref[j] = total.astype(jnp.bfloat16)
        sem = sems.at[lines + j]
        departures.append(pltpu.make_async_copy(out_ref.at[j], out_hbm.at[j], sem))
        departures[j].start()
    for copy in departures:
        copy.wait()


def combine_kernel(part_ref, out_ref):
    tokens = out_ref.shape[0]
    each = part_ref.shape[0] // HK
    for g in range(HK):
        for kind in range(2):
            rows = slice(kind * tokens, (kind + 1) * tokens)
            total = part_ref[g * each, rows, :].astype(jnp.float32)
            for j in range(g * each + 1, (g + 1) * each):
                total += part_ref[j, rows, :].astype(jnp.float32)
            at = (kind * HK + g) * DH
            out_ref[:, at : at + DH] = total.astype(jnp.bfloat16)


def weight_kernel(*refs):
    cols_hbm, (kv_hbm, out_hbm, cols_ref, kv_ref, out_ref, sems) = refs[:-6], refs[-6:]
    mine = lax.axis_index("dp")
    dp = len(cols_hbm)
    seq, share = out_ref.shape[0], out_ref.shape[1]
    pieces = 4
    some = seq // pieces
    rows = some * share
    first = pltpu.make_async_copy(kv_hbm, kv_ref, sems.at[0])
    first.start()
    arrivals, departures = [], []
    for j in range(pieces):
        at, to = pl.ds(j * rows, rows), pl.ds(j * some, some)
        for r in range(dp):
            sem = sems.at[1 + j * dp + r]
            arrivals.append(
                pltpu.make_async_copy(cols_hbm[r].at[at], cols_ref.at[r, at], sem)
            )
        sem = sems.at[1 + pieces * dp + j]
        departures.append(pltpu.make_async_copy(out_ref.at[to], out_hbm.at[to], sem))
    for copy in arrivals:
        copy.start()
    first.wait()
    for j in range(pieces):
        total = None
        for r in range(dp):
            arrivals[j * dp + r].wait()
            part = dot(
                cols_ref[r, j * rows : (j + 1) * rows], kv_ref[jnp.bitwise_xor(mine, r)], NN
            )
            total = part if total is None else total + part
        out_ref[j * some : (j + 1) * some] = total.astype(jnp.bfloat16).reshape(
            some, share, total.shape[1]
        )
        departures[j].start()
    for copy in departures:
        copy.wait()


def unpack_kernel(*refs):
    part_hbm, out_hbm, part_ref, out_ref, sems = refs[:-4], *refs[-4:]
    line = lax.axis_index("seq") // PLANES
    heads = part_ref.shape[1]
    arrivals = [
        pltpu.make_async_copy(part, part_ref.at[k], sems.at[k]) for k, part in enumerate(part_hbm)
    ]
    for copy in arrivals:
        copy.start()
    for k, copy in enumerate(arrivals):
        copy.wait()
        first = jnp.bitwise_xor(line, k) * heads
        for h in range(heads):
            at = pl.ds(pl.multiple_of((first + h) * DH, DH), DH)
            out_ref[:, at] = part_ref[k, h]
    copy = pltpu.make_async_copy(out_ref, out_hbm, sems.at[len(part_hbm)])
    copy.start()
    copy.wait()


def total_kernel(part_hbm, out_hbm, part_ref, out_ref, sems):
    seq = part_ref.shape[0]
    pieces = sems.shape[0] - 1
    some = seq // pieces
    arrivals = []
    for j in range(pieces):
        at = pl.ds(j * some, some)
        arrivals.append(pltpu.make_async_copy(part_hbm.at[at], part_ref.at[at], sems.at[j]))
    for copy in arrivals:
        copy.start()
    total = jnp.zeros(out_ref.shape, jnp.float32)
    for j in range(pieces):
        arrivals[j].wait()
        for s in range(j * some, (j + 1) * some):
            total += part_ref[s].astype(jnp.float32)
    out_ref[...] = total
    copy = pltpu.make_async_copy(out_ref, out_hbm, sems.at[pieces])
    copy.start()
    copy.wait()


def exchange(array, axis, groups=None):
    return lax.all_to_all(
        array, axis, split_axis=0, concat_axis=0, axis_index_groups=groups, tiled=True
    )


def shards(hidden, queries, keyvals, out_grad, segment):
    seq, dp = lax.axis_size("seq"), lax.axis_size("dp")
    tokens, width = hidden.shape[1], hidden.shape[2]
    share = width // (seq * dp)
    lines = seq // PLANES
    heads = HQ // lines
    half = jnp.bfloat16
    shape = jax.ShapeDtypeStruct
    along = [[j * PLANES + w for j in range(lines)] for w in range(PLANES)]
    across = [[j * PLANES + w for w in range(PLANES)] for j in range(lines)]

    def partners(k):
        return [(p, (p // PLANES ^ k) * PLANES + p % PLANES) for p in range(seq)]

    shared = (lines, 2 * tokens + SEGMENT_ROWS, DH)
    kv = local(
        share_kernel,
        shape(shared, half),
        [keyvals[0], segment],
        [
            pltpu.VMEM(keyvals.shape[1:], half),
            pltpu.VMEM(segment.shape, segment.dtype),
            pltpu.VMEM(shared, half),
            pltpu.SemaphoreType.DMA((3,)),
        ],
        "share",
    )
    parts = local(
        pack_kernel,
        (shape((2 * heads, tokens, DH), half),) * lines
        + (shape((seq * share, tokens), half),) * dp,
        [queries[0], out_grad[0], hidden[0]],
        [
            pltpu.VMEM(queries.shape[1:], half),
            pltpu.VMEM(out_grad.shape[1:], half),
            pltpu.VMEM(hidden.shape[1:], half),
            pltpu.VMEM((lines, 2 * heads, tokens, DH), half),
            pltpu.VMEM((dp, seq * share, tokens), half),
            pltpu.SemaphoreType.DMA((3,)),
            pltpu.SemaphoreType.DMA((lines + dp,)),
        ],
        "pack",
    )
    parts, columns = list(parts[:lines]), list(parts[lines:])
    kv, parts = lax.optimization_barrier((exchange(kv, "seq", along), parts))
    for k in range(1, lines):
        parts[k] = lax.ppermute(parts[k], "seq", partners(k))
    kv = jnp.broadcast_to(kv[None], (PLANES,) + shared)
    kv = exchange(kv, "seq", across)
    kv, parts, columns = lax.optimization_barrier((kv, parts, columns))
    for k in range(1, dp):
        columns[k] = lax.ppermute(columns[k], "dp", [(r, r ^ k) for r in range(dp)])
    dkv, *dq = attention(kv, parts)
    dkv, dq, columns = lax.optimization_barrier((dkv, dq, columns))
    for k in range(1, lines):
        dq[k] = lax.ppermute(dq[k], "seq", partners(k))
    dkv, dq = lax.optimization_barrier((exchange(dkv, "seq", across), dq))
    dkv = local(
        gather_kernel,
        shape((lines, 2 * tokens, DH), half),
        [dkv],
        [
            pltpu.VMEM(dkv.shape, half),
            pltpu.VMEM(dkv.shape[1:], half),
            pltpu.SemaphoreType.DMA((2 * lines,)),
        ],
        "gather",
    )
    dkv = exchange(dkv, "seq", along)
    keyval_grad = pl.pallas_call(
        combine_kernel,
        out_shape=shape((tokens, 2 * HK * DH), half),
        in_specs=[pl.BlockSpec(memory_space=pltpu.VMEM)],
        out_specs=pl.BlockSpec(memory_space=pltpu.VMEM),
        compiler_params=pltpu.CompilerParams(vmem_limit_bytes=SMALL_LIMIT),
        name="combine",
    )(dkv)
    every = lax.all_gather(keyval_grad, "dp", axis=0)
    result = (seq, share, 2 * HK * DH)
    partial = local(
        weight_kernel,
        shape(result, half),
        [*columns, every],
        [
            pltpu.VMEM((dp, seq * share, tokens), half),
            pltpu.VMEM(every.shape, half),
            pltpu.VMEM(result, half),
            pltpu.SemaphoreType.DMA((1 + 4 * dp + 4,)),
        ],
        "weight",
    )
    partial = exchange(partial, "seq")
    query_grad = local(
        unpack_kernel,
        shape((tokens, HQ * DH), half),
        dq,
        [
            pltpu.VMEM((lines, heads, tokens, DH), half),
            pltpu.VMEM((tokens, HQ * DH), half),
            pltpu.SemaphoreType.DMA((lines + 1,)),
        ],
        "unpack",
    )
    weight_grad = local(
        total_kernel,
        shape(result[1:], jnp.float32),
        [partial],
        [
            pltpu.VMEM(result, half),
            pltpu.VMEM(result[1:], jnp.float32),
            pltpu.SemaphoreType.DMA((5,)),
        ],
        "total",
    )
    return (query_grad[None], keyval_grad[None], weight_grad)


def solution(mesh):
    in_specs = (
        P("dp", "seq", None),
        P("dp", "seq", None),
        P("dp", "seq", None),
        P("dp", "seq", None),
        P("dp", "seq"),
    )
    out_specs = (P("dp", "seq", None), P("dp", "seq", None), P(("seq", "dp"), None))
    return jax.shard_map(shards, mesh=mesh, in_specs=in_specs, out_specs=out_specs, check_vma=False)
```

```python
import jax
import jax.numpy as jnp
from jax import lax
from jax.experimental import pallas as pl
from jax.experimental.pallas import tpu as pltpu
from jax.sharding import PartitionSpec as P

HQ = 32
HK = 2
DH = 128
SCALE = DH ** -0.5
EXP2_SCALE = SCALE * 1.4426950408889634
MASKED = -1e30
LOWEST = -1e29
SEGMENT_ROWS = 16
BQ = 1024
UNIT = 256
CHUNKS = (4, 2, 1)
PLANES = 8
VMEM_LIMIT = 127 * 512 * 1024
SMALL_LIMIT = 20 * 1024 * 1024
ATTENTION_LIMIT = 59 * 1024 * 1024
NT = (((1,), (1,)), ((), ()))
NN = (((1,), (0,)), ((), ()))


def dot(a, b, dims):
    return lax.dot_general(a, b, dims, preferred_element_type=jnp.float32)


def attention_kernel(*refs):
    kv_hbm, q_hbm = refs[0], refs[1:5]
    dkv_hbm, dq_hbm = refs[5], refs[6:10]
    x_ref, seg_ref, q_ref, dq_ref, dkv_ref = refs[10:15]
    p_ref, dp_ref, m_ref, dk_ref, dv_ref, kt_ref, sems, out_sems = refs[15:]
    planes, lines = kv_hbm.shape[0], kv_hbm.shape[1]
    blocks = planes * lines
    seq = blocks * 128
    un = UNIT // 128
    mine = lax.axis_index("seq")
    line, plane = mine // planes, mine % planes

    arrivals = []
    for j in range(lines):
        at = pl.ds(j * planes, planes)
        arrivals.append(
            pltpu.make_async_copy(kv_hbm.at[:, j, 256:], seg_ref.at[at], sems.at[j])
        )
    for j in range(lines):
        at = pl.ds(j * planes, planes)
        arrivals.append(
            pltpu.make_async_copy(kv_hbm.at[:, j, :256], x_ref.at[at], sems.at[lines + j])
        )
    for j in range(lines):
        arrivals.append(pltpu.make_async_copy(q_hbm[j], q_ref.at[j], sems.at[2 * lines + j]))
    for copy in arrivals:
        copy.start()

    def departure(j):
        return pltpu.make_async_copy(dq_ref.at[j], dq_hbm[j], out_sems.at[j])

    def final(j):
        return pltpu.make_async_copy(dkv_ref.at[:, j], dkv_hbm.at[:, j], out_sems.at[lines + j])

    dk_ref[...] = jnp.zeros_like(dk_ref)
    dv_ref[...] = jnp.zeros_like(dv_ref)
    for copy in arrivals[: 2 * lines]:
        copy.wait()

    def rows(first, count, slot):
        part = x_ref[pl.ds(first, count), slot * 128 : (slot + 1) * 128, :]
        return part.reshape(count * 128, DH)

    def turn(b, _):
        kt_ref[:, pl.ds(pl.multiple_of(b * 128, 128), 128)] = x_ref[b, :128, :].T
        return 0

    lax.fori_loop(0, blocks, turn, 0)
    segments = seg_ref[:, 0:1, :].astype(jnp.float32)
    count0 = jnp.sum(jnp.where(segments < 0.5, 1.0, 0.0)).astype(jnp.int32)
    count1 = jnp.sum(jnp.where(segments < 1.5, 1.0, 0.0)).astype(jnp.int32)

    def start_of(pos):
        return jnp.where(pos >= count1, count1, jnp.where(pos >= count0, count0, 0))

    heads = dq_ref.shape[1]
    some = BQ // 128
    turns = heads // some

    def query_block(i, _):
        j, part = i // turns, i % turns
        for k in range(lines):
            pl.when(i == k * turns)(arrivals[2 * lines + k].wait)
        first = (jnp.bitwise_xor(line, j) * planes + plane) * 128
        q = q_ref[j, pl.ds(part * some, some)].reshape(BQ, DH)
        cotan = q_ref[j, pl.ds(heads + part * some, some)].reshape(BQ, DH)
        qpos = first + lax.broadcasted_iota(jnp.int32, (1, BQ), 1) % 128
        qstart = start_of(qpos)
        low = start_of(first) // UNIT
        high = (first + 127) // UNIT + 1

        def walk(body, state):
            at = low
            for size in CHUNKS:
                count = (high - at) // size

                def step(t, carry, size=size, at=at):
                    return body(at + t * size, size, carry)

                state = lax.fori_loop(0, count, step, state)
                at = at + count * size
            return state

        def scores(kb, size, carry):
            plain = ((kb + size) * UNIT <= first) & (kb * UNIT >= start_of(first + 127))
            return lax.cond(
                plain,
                lambda c: score_part(kb, size, c, False),
                lambda c: score_part(kb, size, c, True),
                carry,
            )

        def score_part(kb, size, carry, masked):
            top, total, delta = carry
            k = rows(kb * un, size * un, 0)
            v = rows(kb * un, size * un, 1)
            st = dot(k, q, NT)
            dpt = dot(v, cotan, NT)
            at = pl.ds(pl.multiple_of(kb * UNIT, UNIT), size * UNIT)
            if masked:
                kpos = kb * UNIT + lax.broadcasted_iota(jnp.int32, (size * UNIT, BQ), 0)
                st = jnp.where((kpos >= qstart) & (kpos <= qpos), st, MASKED)
            newtop = jnp.maximum(top, jnp.max(st, axis=0, keepdims=True))
            p = jnp.exp2((st - newtop) * EXP2_SCALE)
            fade = jnp.exp2((top - newtop) * EXP2_SCALE)
            total = total * fade + jnp.sum(p, axis=0, keepdims=True)
            delta = delta * fade + jnp.sum(p * dpt, axis=0, keepdims=True)
            p_ref[at, :] = p
            dp_ref[at, :] = dpt
            m_ref[pl.ds(kb, 1), :] = newtop
            return newtop, total, delta

        zero = jnp.zeros((1, BQ), jnp.float32)
        top, total, delta = walk(scores, (zero + LOWEST, zero, zero))
        inverse = 1.0 / total
        delta = delta * inverse

        def grads(kb, size, dq):
            at = pl.ds(pl.multiple_of(kb * UNIT, UNIT), size * UNIT)
            factor = jnp.exp2((m_ref[pl.ds(kb, 1), :] - top) * EXP2_SCALE) * inverse
            w = p_ref[at, :] * factor
            ds = (w * (dp_ref[at, :] - delta)).astype(jnp.bfloat16)
            dv_ref[at, :] += dot(w.astype(jnp.bfloat16), cotan, NN)
            dk_ref[at, :] += dot(ds, q, NN)
            return dq + dot(kt_ref[:, at], ds, NN)

        dq = walk(grads, jnp.zeros((DH, BQ), jnp.float32)).T
        dq_ref[j, pl.ds(part * some, some)] = (
            (dq * SCALE).astype(jnp.bfloat16).reshape(some, 128, DH)
        )
        for k in range(lines):
            pl.when(i == (k + 1) * turns - 1)(departure(k).start)
        return 0

    lax.fori_loop(0, lines * turns, query_block, 0)

    def finish(b, _):
        at = pl.ds(pl.multiple_of(b * 128, 128), 128)
        dkv_ref[b % planes, b // planes, :128, :] = (dk_ref[at, :] * SCALE).astype(jnp.bfloat16)
        dkv_ref[b % planes, b // planes, 128:, :] = dv_ref[at, :].astype(jnp.bfloat16)
        return 0

    for j in range(lines):
        lax.fori_loop(j * planes, (j + 1) * planes, finish, 0)
        final(j).start()
    for j in range(lines):
        departure(j).wait()
        final(j).wait()


def local(body, out_shape, inputs, scratch, name, limit=VMEM_LIMIT):
    spec = pl.BlockSpec(memory_space=pltpu.HBM)
    many = isinstance(out_shape, tuple)
    return pl.pallas_call(
        body,
        out_shape=out_shape,
        in_specs=[spec] * len(inputs),
        out_specs=(spec,) * len(out_shape) if many else spec,
        scratch_shapes=scratch,
        compiler_params=pltpu.CompilerParams(vmem_limit_bytes=limit),
        name=name,
    )(*inputs)


def attention(kv, parts):
    planes, lines = kv.shape[0], kv.shape[1]
    blocks = planes * lines
    seq = blocks * 128
    heads = parts[0].shape[0] // 2
    half = jnp.bfloat16
    shape = jax.ShapeDtypeStruct
    spec = pl.BlockSpec(memory_space=pltpu.HBM)
    return pl.pallas_call(
        attention_kernel,
        out_shape=(shape((planes, lines, 256, DH), half),)
        + (shape((heads, 128, DH), half),) * lines,
        in_specs=[spec] * (1 + lines),
        out_specs=(spec,) * (1 + lines),
        scratch_shapes=[
            pltpu.VMEM((blocks, 256, DH), half),
            pltpu.VMEM((blocks, SEGMENT_ROWS, 128), half),
            pltpu.VMEM((lines, 2 * heads, 128, DH), half),
            pltpu.VMEM((lines, heads, 128, DH), half),
            pltpu.VMEM((planes, lines, 256, DH), half),
            pltpu.VMEM((seq, BQ), jnp.float32),
            pltpu.VMEM((seq, BQ), jnp.float32),
            pltpu.VMEM((max(8, seq // UNIT), BQ), jnp.float32),
            pltpu.VMEM((seq, DH), jnp.float32),
            pltpu.VMEM((seq, DH), jnp.float32),
            pltpu.VMEM((DH, seq), half),
            pltpu.SemaphoreType.DMA((3 * lines,)),
            pltpu.SemaphoreType.DMA((2 * lines,)),
        ],
        compiler_params=pltpu.CompilerParams(vmem_limit_bytes=ATTENTION_LIMIT),
        cost_estimate=pl.CostEstimate(
            flops=10 * 1000**3, bytes_accessed=8 * 1000**2, transcendentals=8 * 1000**2
        ),
        name="attention",
    )(kv, *parts)


def share_kernel(kv_hbm, seg_hbm, out_hbm, kv_ref, seg_ref, out_ref, sems):
    pairs = [(seg_hbm, seg_ref), (kv_hbm, kv_ref)]
    arrivals = [pltpu.make_async_copy(*pair, sems.at[i]) for i, pair in enumerate(pairs)]
    for copy in arrivals:
        copy.start()
    tokens = kv_ref.shape[0]
    lines = out_ref.shape[0]
    arrivals[0].wait()
    numbers = jnp.broadcast_to(seg_ref[...].astype(jnp.bfloat16), (SEGMENT_ROWS, tokens))
    arrivals[1].wait()
    for j in range(lines):
        k = (j * HK // lines) * DH
        v = HK * DH + k
        out_ref[j, :tokens, :] = kv_ref[:, k : k + DH]
        out_ref[j, tokens : 2 * tokens, :] = kv_ref[:, v : v + DH]
        out_ref[j, 2 * tokens :, :] = numbers
    copy = pltpu.make_async_copy(out_ref, out_hbm, sems.at[2])
    copy.start()
    copy.wait()


def pack_kernel(q_hbm, g_hbm, h_hbm, *rest):
    q_out, cols_out = rest[:4], rest[4:8]
    q_ref, g_ref, h_ref, q_send, cols_ref, in_sems, out_sems = rest[8:]
    line, core = lax.axis_index("seq") // PLANES, lax.axis_index("dp")
    pairs = [(q_hbm, q_ref), (g_hbm, g_ref), (h_hbm, h_ref)]
    arrivals = [pltpu.make_async_copy(*pair, in_sems.at[i]) for i, pair in enumerate(pairs)]
    for copy in arrivals:
        copy.start()
    lines, heads = q_send.shape[0], q_send.shape[1] // 2
    dp, width = cols_ref.shape[0], cols_ref.shape[1]
    share = h_ref.shape[1] // (HQ * dp)
    departures = []
    for k in range(lines):
        departures.append(pltpu.make_async_copy(q_send.at[k], q_out[k], out_sems.at[k]))
    for k in range(dp):
        sem = out_sems.at[lines + k]
        departures.append(pltpu.make_async_copy(cols_ref.at[k], cols_out[k], sem))
    for kind, ref in ((0, q_ref), (1, g_ref)):
        arrivals[kind].wait()
        for h in range(HQ):
            to = jnp.bitwise_xor(line, h // heads)
            q_send[to, kind * heads + h % heads] = ref[:, h * DH : (h + 1) * DH]
    for copy in departures[:lines]:
        copy.start()
    arrivals[2].wait()
    span = share * dp
    for s in range(width // share):
        turned = h_ref[:, s * span : (s + 1) * span].T
        for r in range(dp):
            part = turned[r * share : (r + 1) * share]
            cols_ref[jnp.bitwise_xor(core, r), s * share : (s + 1) * share, :] = part
    for copy in departures[lines:]:
        copy.start()
    for copy in departures:
        copy.wait()


def gather_kernel(part_hbm, out_hbm, part_ref, out_ref, sems):
    planes, lines = part_ref.shape[0], part_ref.shape[1]
    arrivals = [
        pltpu.make_async_copy(part_hbm.at[:, j], part_ref.at[:, j], sems.at[j])
        for j in range(lines)
    ]
    for copy in arrivals:
        copy.start()
    departures = []
    for j in range(lines):
        arrivals[j].wait()
        total = part_ref[0, j].astype(jnp.float32)
        for w in range(1, planes):
            total += part_ref[w, j].astype(jnp.float32)
        out_ref[j] = total.astype(jnp.bfloat16)
        sem = sems.at[lines + j]
        departures.append(pltpu.make_async_copy(out_ref.at[j], out_hbm.at[j], sem))
        departures[j].start()
    for copy in departures:
        copy.wait()


def combine_kernel(part_ref, out_ref):
    tokens = out_ref.shape[0]
    each = part_ref.shape[0] // HK
    for g in range(HK):
        for kind in range(2):
            rows = slice(kind * tokens, (kind + 1) * tokens)
            total = part_ref[g * each, rows, :].astype(jnp.float32)
            for j in range(g * each + 1, (g + 1) * each):
                total += part_ref[j, rows, :].astype(jnp.float32)
            at = (kind * HK + g) * DH
            out_ref[:, at : at + DH] = total.astype(jnp.bfloat16)


def weight_kernel(*refs):
    cols_hbm, (kv_hbm, out_hbm, cols_ref, kv_ref, out_ref, sems) = refs[:-6], refs[-6:]
    mine = lax.axis_index("dp")
    dp = len(cols_hbm)
    seq, share = out_ref.shape[0], out_ref.shape[1]
    pieces = 4
    some = seq // pieces
    rows = some * share
    first = pltpu.make_async_copy(kv_hbm, kv_ref, sems.at[0])
    first.start()
    arrivals, departures = [], []
    for j in range(pieces):
        at, to = pl.ds(j * rows, rows), pl.ds(j * some, some)
        for r in range(dp):
            sem = sems.at[1 + j * dp + r]
            arrivals.append(
                pltpu.make_async_copy(cols_hbm[r].at[at], cols_ref.at[r, at], sem)
            )
        sem = sems.at[1 + pieces * dp + j]
        departures.append(pltpu.make_async_copy(out_ref.at[to], out_hbm.at[to], sem))
    for copy in arrivals:
        copy.start()
    first.wait()
    for j in range(pieces):
        total = None
        for r in range(dp):
            arrivals[j * dp + r].wait()
            part = dot(
                cols_ref[r, j * rows : (j + 1) * rows], kv_ref[jnp.bitwise_xor(mine, r)], NN
            )
            total = part if total is None else total + part
        out_ref[j * some : (j + 1) * some] = total.astype(jnp.bfloat16).reshape(
            some, share, total.shape[1]
        )
        departures[j].start()
    for copy in departures:
        copy.wait()


def unpack_kernel(*refs):
    part_hbm, out_hbm, part_ref, out_ref, sems = refs[:-4], *refs[-4:]
    line = lax.axis_index("seq") // PLANES
    heads = part_ref.shape[1]
    arrivals = [
        pltpu.make_async_copy(part, part_ref.at[k], sems.at[k]) for k, part in enumerate(part_hbm)
    ]
    for copy in arrivals:
        copy.start()
    for k, copy in enumerate(arrivals):
        copy.wait()
        first = jnp.bitwise_xor(line, k) * heads
        for h in range(heads):
            at = pl.ds(pl.multiple_of((first + h) * DH, DH), DH)
            out_ref[:, at] = part_ref[k, h]
    copy = pltpu.make_async_copy(out_ref, out_hbm, sems.at[len(part_hbm)])
    copy.start()
    copy.wait()


def total_kernel(part_ref, out_ref):
    total = part_ref[0].astype(jnp.float32)
    for s in range(1, part_ref.shape[0]):
        total += part_ref[s].astype(jnp.float32)
    out_ref[...] = total


def exchange(array, axis, groups=None):
    return lax.all_to_all(
        array, axis, split_axis=0, concat_axis=0, axis_index_groups=groups, tiled=True
    )


def shards(hidden, queries, keyvals, out_grad, segment):
    seq, dp = lax.axis_size("seq"), lax.axis_size("dp")
    tokens, width = hidden.shape[1], hidden.shape[2]
    share = width // (seq * dp)
    lines = seq // PLANES
    heads = HQ // lines
    half = jnp.bfloat16
    shape = jax.ShapeDtypeStruct
    along = [[j * PLANES + w for j in range(lines)] for w in range(PLANES)]
    across = [[j * PLANES + w for w in range(PLANES)] for j in range(lines)]

    def partners(k):
        return [(p, (p // PLANES ^ k) * PLANES + p % PLANES) for p in range(seq)]

    shared = (lines, 2 * tokens + SEGMENT_ROWS, DH)
    kv = local(
        share_kernel,
        shape(shared, half),
        [keyvals[0], segment],
        [
            pltpu.VMEM(keyvals.shape[1:], half),
            pltpu.VMEM(segment.shape, segment.dtype),
            pltpu.VMEM(shared, half),
            pltpu.SemaphoreType.DMA((3,)),
        ],
        "share",
    )
    parts = local(
        pack_kernel,
        (shape((2 * heads, tokens, DH), half),) * lines
        + (shape((seq * share, tokens), half),) * dp,
        [queries[0], out_grad[0], hidden[0]],
        [
            pltpu.VMEM(queries.shape[1:], half),
            pltpu.VMEM(out_grad.shape[1:], half),
            pltpu.VMEM(hidden.shape[1:], half),
            pltpu.VMEM((lines, 2 * heads, tokens, DH), half),
            pltpu.VMEM((dp, seq * share, tokens), half),
            pltpu.SemaphoreType.DMA((3,)),
            pltpu.SemaphoreType.DMA((lines + dp,)),
        ],
        "pack",
    )
    parts, columns = list(parts[:lines]), list(parts[lines:])
    kv, parts = lax.optimization_barrier((exchange(kv, "seq", along), parts))
    for k in range(1, lines):
        parts[k] = lax.ppermute(parts[k], "seq", partners(k))
    kv = jnp.broadcast_to(kv[None], (PLANES,) + shared)
    kv = exchange(kv, "seq", across)
    kv, parts, columns = lax.optimization_barrier((kv, parts, columns))
    for k in range(1, dp):
        columns[k] = lax.ppermute(columns[k], "dp", [(r, r ^ k) for r in range(dp)])
    dkv, *dq = attention(kv, parts)
    dkv, dq, columns = lax.optimization_barrier((dkv, dq, columns))
    for k in range(1, lines):
        dq[k] = lax.ppermute(dq[k], "seq", partners(k))
    dkv, dq = lax.optimization_barrier((exchange(dkv, "seq", across), dq))
    dkv = local(
        gather_kernel,
        shape((lines, 2 * tokens, DH), half),
        [dkv],
        [
            pltpu.VMEM(dkv.shape, half),
            pltpu.VMEM(dkv.shape[1:], half),
            pltpu.SemaphoreType.DMA((2 * lines,)),
        ],
        "gather",
    )
    dkv = exchange(dkv, "seq", along)
    keyval_grad = pl.pallas_call(
        combine_kernel,
        out_shape=shape((tokens, 2 * HK * DH), half),
        in_specs=[pl.BlockSpec(memory_space=pltpu.VMEM)],
        out_specs=pl.BlockSpec(memory_space=pltpu.VMEM),
        compiler_params=pltpu.CompilerParams(vmem_limit_bytes=SMALL_LIMIT),
        name="combine",
    )(dkv)
    every = lax.all_gather(keyval_grad, "dp", axis=0)
    result = (seq, share, 2 * HK * DH)
    partial = local(
        weight_kernel,
        shape(result, half),
        [*columns, every],
        [
            pltpu.VMEM((dp, seq * share, tokens), half),
            pltpu.VMEM(every.shape, half),
            pltpu.VMEM(result, half),
            pltpu.SemaphoreType.DMA((1 + 4 * dp + 4,)),
        ],
        "weight",
    )
    partial = exchange(partial, "seq")
    query_grad = local(
        unpack_kernel,
        shape((tokens, HQ * DH), half),
        dq,
        [
            pltpu.VMEM((lines, heads, tokens, DH), half),
            pltpu.VMEM((tokens, HQ * DH), half),
            pltpu.SemaphoreType.DMA((lines + 1,)),
        ],
        "unpack",
        SMALL_LIMIT,
    )
    weight_grad = pl.pallas_call(
        total_kernel,
        out_shape=shape(result[1:], jnp.float32),
        in_specs=[pl.BlockSpec(memory_space=pltpu.VMEM)],
        out_specs=pl.BlockSpec(memory_space=pltpu.VMEM),
        compiler_params=pltpu.CompilerParams(vmem_limit_bytes=SMALL_LIMIT),
        name="total",
    )(partial)
    return (query_grad[None], keyval_grad[None], weight_grad)


def solution(mesh):
    in_specs = (
        P("dp", "seq", None),
        P("dp", "seq", None),
        P("dp", "seq", None),
        P("dp", "seq", None),
        P("dp", "seq"),
    )
    out_specs = (P("dp", "seq", None), P("dp", "seq", None), P(("seq", "dp"), None))
    return jax.shard_map(shards, mesh=mesh, in_specs=in_specs, out_specs=out_specs, check_vma=False)
```
